32 devices in a mesh: dom: 8 (over z, core), sub: 4 (over y, x).
Axes of the slice: x: 2, y: 2, z: 4, core: 2. Of those that a mesh axis runs over, the one named last changes fastest.
Arguments:
- coupling: bfloat16 [256, 6, 128, 128], P(('dom', 'sub')), may hold values from -0.25 to 0.25
- diag_inv: bfloat16 [256, 128, 128], P(('dom', 'sub')), may hold values from -0.5 to 0.5
- rhs: float32 [256, 64, 128], P(('dom', 'sub')), may hold values from -6 to 6
- color: int32 [256], P(('dom', 'sub')), may hold values from 0 to 3, as said below
- local_target: int32 [256, 2], P(('dom', 'sub')), may hold values from 0 to 7, as said below
- group_peer: int32 [256, 2], P(('dom', 'sub')), may hold values from 0 to 3, as said below
- group_list: int32 [32, 4, 4], P(('dom', 'sub')), may hold values from -1 to 7, as said below
- dom_target: int32 [256, 2], P(('dom', 'sub')), may hold values from 0 to 7, as said below
Outputs:
- solution: float32 [256, 64, 128], P(('dom', 'sub'))
- defect: float32 [256, 64, 128], P(('dom', 'sub'))
The draws below stay inside these ranges and needn't reach their ends.
Inputs may be any that keep to these rules, and one draw needn't show every extreme that they name: Each partition window of 8 consecutive block rows holds exactly a quarter of its rows of each color. `local_target`: A row of another color than row i, in the same partition window. `group_peer`: never the row's own member of the group; the two entries of a row differ. `group_list`: entry [p, c, q] is the local index on member q of p's group of a row of another color than c that receives all of p's color-c couplings to q, and -1 where p has none; a partition sends at most one row's sum to each member in a color. `dom_target`: groups form a cycle; the row reached is always of another color than row i.
All inputs are finite; a program needn't handle non-finite values.
Results may differ from the reference program's by a relative error of at most 0.012.
Values sent between devices are 32-bit elements; how exact they have to be, the bound alone decides.
No kernel may reach another device: no remote copies, remote signals or barrier semaphores. Data moves between devices by JAX's collectives and lax.ppermute only.
A program may use at most 64 MiB of HBM per device.

```python
import jax
import jax.numpy as jnp
from jax import lax

B = 128
NRHS = 64
ROWS_DEV = 8
COLORS = 4
SWEEPS = 2
COUPLINGS = 6
GROUP = 4
NPART = 32
NROWS = 256


def pattern(base_key):
    quarter = ROWS_DEV // 4
    groups = NPART // GROUP
    subkeys = jax.random.split(base_key, 8)
    scores = jax.random.randint(subkeys[0], (NPART, ROWS_DEV), 0, 1 << 20) * ROWS_DEV + jnp.arange(ROWS_DEV, dtype=jnp.int32)[None, :]
    shuffle = jnp.argsort(scores, axis=1).astype(jnp.int32)
    inverse = jnp.argsort(shuffle, axis=1).astype(jnp.int32)
    row_color = (shuffle // quarter).astype(jnp.int32)
    rows_of = inverse.reshape(NPART, 4, quarter)

    def pick(seed_key, part_index, avoid):
        first_key, second_key = jax.random.split(seed_key)
        other_color = (avoid + jax.random.randint(first_key, avoid.shape, 1, 4)) % 4
        position = jax.random.randint(second_key, avoid.shape, 0, quarter)
        part_full = jnp.broadcast_to(part_index, avoid.shape)
        return rows_of[part_full, other_color, position].astype(jnp.int32)
    part_ids = jnp.arange(NPART, dtype=jnp.int32)[:, None]
    group_of = part_ids // GROUP
    member = part_ids % GROUP
    local_rows = pick(subkeys[1], part_ids[:, :, None], jnp.broadcast_to(row_color[:, :, None], (NPART, ROWS_DEV, 2)))
    up_part = (group_of + 1) % groups * GROUP + member
    down_part = (group_of - 1 + groups) % groups * GROUP + member
    up_rows = pick(subkeys[2], up_part, row_color)
    down_rows = pick(subkeys[3], down_part, row_color)
    dom_rows = jnp.stack([up_rows, down_rows], axis=-1)
    busiest = jax.random.randint(subkeys[4], (groups, 4), 0, GROUP)
    busiest_row = busiest[jnp.broadcast_to(group_of, (NPART, ROWS_DEV)), row_color]
    first_off = jax.random.randint(subkeys[5], (NPART, ROWS_DEV), 1, GROUP)
    leading = shuffle % quarter == 0
    forced = (busiest_row - member) % GROUP
    first_off = jnp.where(leading & (forced != 0), forced, first_off)
    second_off = 1 + (first_off - 1 + jax.random.randint(subkeys[6], (NPART, ROWS_DEV), 1, GROUP - 1)) % (GROUP - 1)
    peer_ids = ((member[:, :, None] + jnp.stack([first_off, second_off], axis=-1)) % GROUP).astype(jnp.int32)
    color_ids = jnp.arange(4, dtype=jnp.int32)
    members = jnp.arange(GROUP, dtype=jnp.int32)
    in_use = jnp.any((row_color[:, :, None, None, None] == color_ids[None, None, None, :, None]) & (peer_ids[:, :, :, None, None] == members[None, None, None, None, :]), axis=(1, 2))
    dest_part = jnp.broadcast_to((group_of * GROUP + members[None, :])[:, None, :], (NPART, 4, GROUP))
    dest_rows = pick(subkeys[7], dest_part, jnp.broadcast_to(color_ids[None, :, None], (NPART, 4, GROUP)))
    send_list = jnp.where(in_use, dest_rows, -1).astype(jnp.int32)
    return (row_color.reshape(-1), local_rows.reshape(-1, 2), peer_ids.reshape(-1, 2), send_list, dom_rows.reshape(-1, 2))


def draw_color(key, part):
    return pattern(jax.random.fold_in(key, 4021))[0]


def draw_local_target(key, part):
    return pattern(jax.random.fold_in(key, 4021))[1]


def draw_group_peer(key, part):
    return pattern(jax.random.fold_in(key, 4021))[2]


def draw_group_list(key, part):
    return pattern(jax.random.fold_in(key, 4021))[3]


def draw_dom_target(key, part):
    return pattern(jax.random.fold_in(key, 4021))[4]


def block_levels(own_key, dims, cuts, least, high):
    level, own = 1.0, jax.random.fold_in(own_key, 6)
    for dim, blocks in cuts:
        steps = jnp.exp(jax.random.uniform(jax.random.fold_in(own, dim), (blocks,), jnp.float32, least / len(cuts), high / len(cuts)))
        level = level * jnp.repeat(steps, dims[dim] // blocks).reshape([-1 if axis == dim else 1 for axis in range(len(dims))])
    return level


def bell_draw(key, dims, width, most, cuts=(), kind=jnp.bfloat16):
    factor_of = block_levels(key, dims, cuts, -0.22, 0.18) if cuts else 1.0
    result = jax.random.normal(key, dims, jnp.float32) * width * factor_of
    return jnp.minimum(jnp.maximum(result, -most), most).astype(kind)


def setup_inputs(seed: int = 0) -> dict:
    seeds = jax.random.split(jax.random.key(seed), 9)
    return {
        "coupling": bell_draw(seeds[0], (NROWS, COUPLINGS, B, B), (4 * B) ** -0.5, 0.25, ((0, 32),)),
        "diag_inv": bell_draw(seeds[1], (NROWS, B, B), B ** -0.5, 0.5, ((0, 32),)),
        "rhs": bell_draw(seeds[2], (NROWS, NRHS, B), 1.0, 6.0, ((0, 32),), jnp.float32),
        "color": draw_color(jax.random.fold_in(seeds[8], 71), 0),
        "local_target": draw_local_target(jax.random.fold_in(seeds[8], 71), 0),
        "group_peer": draw_group_peer(jax.random.fold_in(seeds[8], 71), 0),
        "group_list": draw_group_list(jax.random.fold_in(seeds[8], 71), 0),
        "dom_target": draw_dom_target(jax.random.fold_in(seeds[8], 71), 0),
    }


def reference(coupling, diag_inv, rhs, color, local_target, group_peer, group_list, dom_target):
    row_count = rhs.shape[0]
    row_index = jnp.arange(row_count, dtype=jnp.int32)
    partition = row_index // ROWS_DEV
    group_of = partition // GROUP
    member = partition % GROUP
    groups = NPART // GROUP
    local_rows = partition[:, None] * ROWS_DEV + local_target
    peer_rows = group_list[partition[:, None], color[:, None], group_peer]
    group_rows = (group_of[:, None] * GROUP + group_peer) * ROWS_DEV + peer_rows
    up_rows = (((group_of + 1) % groups) * GROUP + member) * ROWS_DEV + dom_target[:, 0]
    down_rows = (((group_of - 1 + groups) % groups) * GROUP + member) * ROWS_DEV + dom_target[:, 1]
    targets = jnp.concatenate([local_rows, group_rows, up_rows[:, None], down_rows[:, None]], axis=1).astype(jnp.int32)
    by_color = jnp.argsort(color, stable=True).astype(jnp.int32).reshape(COLORS, row_count // COLORS)
    solution = jnp.zeros(rhs.shape, jnp.float32)
    coupled = jnp.zeros(rhs.shape, jnp.float32)
    for sweep_no in range(SWEEPS):
        for color_now in range(COLORS):
            picked = by_color[color_now]
            update_in = (rhs[picked] - coupled[picked]).astype(jnp.bfloat16)
            updated = jnp.einsum("prb,pbe->pre", update_in.astype(jnp.float32), diag_inv[picked].astype(jnp.float32), precision=lax.Precision.HIGHEST)
            change = (updated - solution[picked]).astype(jnp.bfloat16)
            solution = solution.at[picked].set(updated)
            products = jnp.einsum("prb,pkbe->pkre", change.astype(jnp.float32), coupling[picked].astype(jnp.float32), precision=lax.Precision.HIGHEST)
            flat_products = products.reshape(-1, rhs.shape[1], rhs.shape[2])
            coupled = coupled + jax.ops.segment_sum(flat_products, targets[picked].reshape(-1), num_segments=row_count)
    return solution, rhs - coupled
```

```python
import functools

import jax
import jax.numpy as jnp
from jax import lax
from jax.experimental import pallas as pl
from jax.experimental.pallas import tpu as pltpu
from jax.sharding import PartitionSpec as P

COLORS = 4
SWEEPS = 2
COUPLINGS = 6
META = 8

VMEM = pl.BlockSpec(memory_space=pltpu.VMEM)
SMEM = pl.BlockSpec(memory_space=pltpu.SMEM)


def is_pow2(n):
    return n & (n - 1) == 0


def partner(member, shift, size):
    if is_pow2(size):
        return member ^ shift
    return lax.rem(member + shift, size)


def slot_of(member, peer, size):
    if is_pow2(size):
        return (member ^ peer) - 1
    return lax.rem(peer - member + size, size) - 1


def dot(a, b):
    return jnp.dot(a, b, preferred_element_type=jnp.float32)


class Sizes:
    def __init__(self, rows, rhs_count, width, group):
        self.rows, self.n, self.w, self.group = rows, rhs_count, width, group
        self.quarter = rows // COLORS
        self.slots = group - 1
        self.order = 0
        self.local = rows
        self.slot = 3 * rows
        self.table = 5 * rows
        self.dom_meta = -(-rows // 8) * 8


def items_of(sz, color, first, got_group, got_up, got_down, meta):
    metas_group, meta_up, meta_down = meta
    out = []
    for s in range(sz.slots):
        out.append((metas_group[s], sz.n + color, got_group[s], 0))
    for ref, got in ((meta_up, got_up), (meta_down, got_down)):
        for p in range(sz.quarter):
            out.append((ref, sz.quarter * sz.n + color * sz.quarter + p, got, p * sz.n))
    return out


def subtract(sz, value, row, items):
    for meta, at, got, start in items:
        here = meta[pl.ds(at, 1), :] == row
        value = value - jnp.where(here, got[pl.ds(start, sz.n), :], 0.0)
    return value


def products(sz, color, table, changes, coupling, send_group, send_up, send_down):
    group_terms = []
    for p in range(sz.quarter):
        at = color * sz.quarter + p
        j = table[sz.order + at]
        pair = jnp.concatenate([coupling[j, 4], coupling[j, 5]], axis=1)
        both = dot(changes[p], pair)
        send_up[pl.ds(p * sz.n, sz.n), :] = both[:, : sz.w]
        send_down[pl.ds(p * sz.n, sz.n), :] = both[:, sz.w :]
        pair = jnp.concatenate([coupling[j, 2], coupling[j, 3]], axis=1)
        both = dot(changes[p], pair)
        for k in range(2):
            group_terms.append((table[sz.slot + 2 * at + k], both[:, k * sz.w : (k + 1) * sz.w]))
    for s in range(sz.slots):
        total = jnp.zeros((sz.n, sz.w), jnp.float32)
        for slot, term in group_terms:
            total = total + jnp.where(slot == s, term, 0.0)
        send_group[s][pl.ds(0, sz.n), :] = total


def first_kernel(sz, color, local_target, group_peer, group_list, dom_target, rhs, diag, coupling, *outs):
    table, sol, change = outs[:3]
    send_up, send_down = outs[3:5]
    send_group = outs[5:]
    me = lax.axis_index("sub")
    colors = [color[i] for i in range(sz.rows)]
    for i in range(sz.rows):
        before = jnp.int32(0)
        for e in range(i):
            before = before + (colors[e] == colors[i]).astype(jnp.int32)
        at = colors[i] * sz.quarter + before
        table[sz.order + at] = i
        for k in range(2):
            table[sz.local + 2 * at + k] = local_target[i, k]
            table[sz.slot + 2 * at + k] = slot_of(me, group_peer[i, k], sz.group)
    changes = []
    for p in range(sz.quarter):
        j = table[sz.order + p]
        new = dot(rhs[j].astype(jnp.bfloat16), diag[j])
        sol[p] = new
        changes.append(new.astype(jnp.bfloat16))
        change[p] = changes[p]
    products(sz, 0, table, changes, coupling, send_group, send_up, send_down)
    line = lax.broadcasted_iota(jnp.int32, (META, sz.w), 0)
    for s in range(sz.slots):
        q = partner(me, s + 1, sz.group)
        meta = jnp.full((META, sz.w), -1, jnp.int32)
        for c in range(COLORS):
            meta = jnp.where(line == c, group_list[0, c, q], meta)
        send_group[s][pl.ds(sz.n, META), :] = meta.astype(jnp.float32)
    line = lax.broadcasted_iota(jnp.int32, (sz.dom_meta, sz.w), 0)
    for k, send in enumerate((send_up, send_down)):
        meta = jnp.full((sz.dom_meta, sz.w), -1, jnp.int32)
        for at in range(sz.rows):
            meta = jnp.where(line == at, dom_target[table[sz.order + at], k], meta)
        send[pl.ds(sz.quarter * sz.n, sz.dom_meta), :] = meta.astype(jnp.float32)


def split_got(sz, refs):
    up, down = refs[:2]
    return refs[2 : 2 + sz.slots], up, down


def step_kernel(sz, color, prev_color, has_old, table, resid, diag, coupling, *refs):
    lanes = 2 + sz.slots
    got, refs = refs[:lanes], refs[lanes:]
    meta, refs = refs[:lanes], refs[lanes:]
    if has_old:
        old, refs = refs[0], refs[1:]
    sol, change, send_up, send_down = refs[:4]
    send_group = refs[4:]
    items = items_of(sz, prev_color, False, *split_got(sz, got), split_got(sz, meta))
    changes = []
    for p in range(sz.quarter):
        j = table[sz.order + color * sz.quarter + p]
        value = subtract(sz, resid[j], j.astype(jnp.float32), items)
        new = dot(value.astype(jnp.bfloat16), diag[j])
        sol[p] = new
        if has_old:
            new = new - old[p]
        changes.append(new.astype(jnp.bfloat16))
        change[p] = changes[p]
    products(sz, color, table, changes, coupling, send_group, send_up, send_down)


def local_kernel(sz, color, prev_color, last, table, resid, coupling, change, *refs):
    lanes = 2 + sz.slots
    items = []
    if prev_color is not None:
        got, refs = refs[:lanes], refs[lanes:]
        meta, refs = refs[:lanes], refs[lanes:]
        items = items_of(sz, prev_color, False, *split_got(sz, got), split_got(sz, meta))
    if last:
        sols, refs = refs[:COLORS], refs[COLORS:]
        out, sol_out = refs
    else:
        (out,) = refs
    for r in range(sz.rows):
        out[r] = subtract(sz, resid[r], jnp.float32(r), items)
    for p in range(sz.quarter):
        at = color * sz.quarter + p
        j = table[sz.order + at]
        both = dot(change[p], jnp.concatenate([coupling[j, 0], coupling[j, 1]], axis=1))
        for k in range(2):
            t = table[sz.local + 2 * at + k]
            out[t] = out[t] - both[:, k * sz.w : (k + 1) * sz.w]
    if last:
        for c in range(COLORS):
            for p in range(sz.quarter):
                sol_out[table[sz.order + c * sz.quarter + p]] = sols[c][p]


def final_kernel(sz, prev_color, resid, *refs):
    lanes = 2 + sz.slots
    got, refs = refs[:lanes], refs[lanes:]
    meta, refs = refs[:lanes], refs[lanes:]
    (out,) = refs
    items = items_of(sz, prev_color, False, *split_got(sz, got), split_got(sz, meta))
    for r in range(sz.rows):
        out[r] = subtract(sz, resid[r], jnp.float32(r), items)


def exchange(sends):
    doms, group = lax.axis_size("dom"), lax.axis_size("sub")
    up = [(i, (i + 1) % doms) for i in range(doms)]
    down = [(j, i) for i, j in up]
    got = [lax.ppermute(sends[0], "dom", up), lax.ppermute(sends[1], "dom", down)]
    for s, send in enumerate(sends[2:]):
        perm = [(i, int(i ^ (s + 1)) if is_pow2(group) else (i + s + 1) % group) for i in range(group)]
        got.append(lax.ppermute(send, "sub", perm))
    return got


def on_device(coupling, diag_inv, rhs, color, local_target, group_peer, group_list, dom_target):
    rows, rhs_count, width = rhs.shape
    sz = Sizes(rows, rhs_count, width, lax.axis_size("sub"))
    f32 = jnp.float32
    sol_t = pltpu.VMEM((sz.quarter, sz.n, sz.w), f32)
    change_t = pltpu.VMEM((sz.quarter, sz.n, sz.w), jnp.bfloat16)

    def send_types(meta_group, meta_dom):
        dom_t = pltpu.VMEM((sz.quarter * sz.n + meta_dom, sz.w), f32)
        return [dom_t, dom_t] + [pltpu.VMEM((sz.n + meta_group, sz.w), f32)] * sz.slots

    params = pltpu.CompilerParams(vmem_limit_bytes=16 * 1024 * 1024)

    def call(body, ins, smem_ins, outs, **kw):
        specs = [SMEM] * smem_ins + [VMEM] * (len(ins) - smem_ins)
        out_specs = [
            SMEM if getattr(o, "memory_space", None) == pltpu.SMEM else VMEM for o in outs
        ]
        return pl.pallas_call(
            body, in_specs=specs, out_specs=out_specs, out_shape=outs, compiler_params=params, **kw
        )(*ins)

    table, sol, change, *sends = call(
        functools.partial(first_kernel, sz),
        [color, local_target, group_peer, group_list, dom_target, rhs, diag_inv, coupling],
        5,
        [pltpu.SMEM((sz.table,), jnp.int32), sol_t, change_t] + send_types(META, sz.dom_meta),
        name="first",
    )
    tiles = pltpu.with_memory_space_constraint(coupling, pltpu.VMEM)
    diags = pltpu.with_memory_space_constraint(diag_inv, pltpu.VMEM)
    sols = [sol]
    resid = rhs
    resid_t = pltpu.VMEM((sz.rows, sz.n, sz.w), f32)
    meta, got = None, None
    steps = SWEEPS * COLORS
    for step in range(steps):
        c, before = step % COLORS, (step - 1) % COLORS
        if step > 0:
            ins = [table, resid, diags, tiles, *got, *meta]
            has_old = step >= COLORS
            if has_old:
                ins.append(sols[c])
            sol, change, *sends = call(
                functools.partial(step_kernel, sz, c, before, has_old),
                ins,
                1,
                [sol_t, change_t] + send_types(0, 0),
                name=f"step{step}",
            )
            if has_old:
                sols[c] = sol
            else:
                sols.append(sol)
        arriving = exchange(sends)
        ins = [table, resid, tiles, change]
        if step > 0:
            ins += [*got, *meta]
        outs = [resid_t]
        last = step == steps - 1
        if last:
            ins += sols
            outs.append(jax.ShapeDtypeStruct(rhs.shape, f32))
        done = call(
            functools.partial(local_kernel, sz, c, before if step > 0 else None, last),
            ins,
            1,
            outs,
            name=f"local{step}",
            input_output_aliases={1: 0} if step > 0 else {},
        )
        resid = done[0]
        got = arriving
        if step == 0:
            meta = got
    (defect,) = call(
        functools.partial(final_kernel, sz, (steps - 1) % COLORS),
        [resid, *got, *meta],
        0,
        [jax.ShapeDtypeStruct(rhs.shape, f32)],
        name="final",
    )
    return done[1], defect


def solution(mesh):
    placed = (
        P(("dom", "sub"), None, None, None),
        P(("dom", "sub"), None, None),
        P(("dom", "sub"), None, None),
        P(("dom", "sub")),
        P(("dom", "sub"), None),
        P(("dom", "sub"), None),
        P(("dom", "sub"), None, None),
        P(("dom", "sub"), None),
    )
    return jax.shard_map(
        on_device,
        mesh=mesh,
        in_specs=placed,
        out_specs=(P(("dom", "sub"), None, None), P(("dom", "sub"), None, None)),
        check_vma=False,
    )
```

```python
import functools

import jax
import jax.numpy as jnp
from jax import lax
from jax.experimental import pallas as pl
from jax.experimental.pallas import tpu as pltpu
from jax.sharding import PartitionSpec as P

COLORS = 4
SWEEPS = 2
META = 8

VMEM = pl.BlockSpec(memory_space=pltpu.VMEM)
SMEM = pl.BlockSpec(memory_space=pltpu.SMEM)
HBM = pl.BlockSpec(memory_space=pltpu.HBM)


def dot(a, b):
    return jnp.dot(a, b, preferred_element_type=jnp.float32)


class Plan:
    def __init__(self, rows, rhs_count, width, group):
        self.rows, self.n, self.w, self.group = rows, rhs_count, width, group
        self.quarter = rows // COLORS
        self.phases = group.bit_length() - 1
        self.lanes = 2 + self.phases
        self.carried = [[s for s in range(1, group) if s >> d & 1] for d in range(self.phases)]
        self.order, self.local, self.slot = 0, rows, 3 * rows
        self.table = 5 * rows
        self.dom_meta = -(-rows // 8) * 8

    def stride(self, step):
        return self.n + (META if step == 0 else 0)

    def at(self, s, phase, step):
        return self.carried[phase].index(s) * self.stride(step)

    def types(self, step):
        dom = self.quarter * self.n + (self.dom_meta if step == 0 else 0)
        shapes = [dom, dom] + [len(c) * self.stride(step) for c in self.carried]
        return [pltpu.VMEM((length, self.w), jnp.float32) for length in shapes]


def items_of(plan, step, got, meta):
    color = step % COLORS
    out = []
    for s in range(1, plan.group):
        d = s.bit_length() - 1
        line = plan.at(s, d, 0) + plan.n + color
        out.append((meta[2 + d], line, got[2 + d], plan.at(s, d, step)))
    for lane in range(2):
        for p in range(plan.quarter):
            line = plan.quarter * plan.n + color * plan.quarter + p
            out.append((meta[lane], line, got[lane], p * plan.n))
    return out


def subtract(plan, value, row, items):
    for meta, line, got, start in items:
        here = meta[pl.ds(line, 1), :] == row
        value = value - jnp.where(here, got[pl.ds(start, plan.n), :], 0.0)
    return value


def products(plan, step, table, changes, coupling, sends):
    parity = lax.rem(lax.axis_index("dom"), 2)
    far, near = sends[:2]
    terms = []
    for p in range(plan.quarter):
        at = step % COLORS * plan.quarter + p
        j = table[plan.order + at]
        both = dot(changes[p], jnp.concatenate([coupling[j, 2], coupling[j, 3]], axis=1))
        for k in range(2):
            terms.append((table[plan.slot + 2 * at + k], both[:, k * plan.w : (k + 1) * plan.w]))
        both = dot(
            changes[p],
            jnp.concatenate([coupling[j, 5 - parity], coupling[j, 4 + parity]], axis=1),
        )
        far[pl.ds(p * plan.n, plan.n), :] = both[:, : plan.w]
        near[pl.ds(p * plan.n, plan.n), :] = both[:, plan.w :]
    for s in range(1, plan.group):
        total = jnp.zeros((plan.n, plan.w), jnp.float32)
        for slot, term in terms:
            total = total + jnp.where(slot == s, term, 0.0)
        d = (s & -s).bit_length() - 1
        sends[2 + d][pl.ds(plan.at(s, d, step), plan.n), :] = total


def first_kernel(plan, *refs):
    hbm, outs, scratch = refs[:8], refs[8 : 14 + plan.lanes], refs[14 + plan.lanes :]
    table, coupling, diag, rhs, sol, change = outs[:6]
    sends = outs[6:]
    color, local_target, group_peer, group_list, dom_target = scratch[:5]
    sems = scratch[5]
    targets = (color, group_peer, group_list, dom_target, local_target, rhs, diag, coupling)
    copies = [
        pltpu.make_async_copy(src, dst, sems.at[i]) for i, (src, dst) in enumerate(zip(hbm, targets))
    ]
    for copy in copies:
        copy.start()
    for copy in copies[:5]:
        copy.wait()
    me = lax.axis_index("sub")
    parity = lax.rem(lax.axis_index("dom"), 2)
    colors = [color[i] for i in range(plan.rows)]
    for i in range(plan.rows):
        before = jnp.int32(0)
        for e in range(i):
            before = before + (colors[e] == colors[i]).astype(jnp.int32)
        at = colors[i] * plan.quarter + before
        table[plan.order + at] = i
        for k in range(2):
            table[plan.local + 2 * at + k] = local_target[k, i]
            table[plan.slot + 2 * at + k] = me ^ group_peer[k, i]
    line = lax.broadcasted_iota(jnp.int32, (META, plan.w), 0)
    for s in range(1, plan.group):
        meta = jnp.full((META, plan.w), -1, jnp.int32)
        for c in range(COLORS):
            meta = jnp.where(line == c, group_list[0, c, me ^ s], meta)
        d = (s & -s).bit_length() - 1
        sends[2 + d][pl.ds(plan.at(s, d, 0) + plan.n, META), :] = meta.astype(jnp.float32)
    line = lax.broadcasted_iota(jnp.int32, (plan.dom_meta, plan.w), 0)
    for send, k in zip(sends[:2], (1 - parity, parity)):
        meta = jnp.full((plan.dom_meta, plan.w), -1, jnp.int32)
        for at in range(plan.rows):
            meta = jnp.where(line == at, dom_target[k, table[plan.order + at]], meta)
        send[pl.ds(plan.quarter * plan.n, plan.dom_meta), :] = meta.astype(jnp.float32)
    copies[5].wait()
    copies[6].wait()
    changes = []
    for p in range(plan.quarter):
        j = table[plan.order + p]
        new = dot(rhs[j].astype(jnp.bfloat16), diag[j])
        sol[p] = new
        changes.append(new.astype(jnp.bfloat16))
        change[p] = changes[p]
    copies[7].wait()
    products(plan, 0, table, changes, coupling, sends)


def step_kernel(plan, step, table, resid, diag, coupling, *refs):
    got, meta, refs = refs[: plan.lanes], refs[plan.lanes : 2 * plan.lanes], refs[2 * plan.lanes :]
    has_old = step >= COLORS
    if has_old:
        old, refs = refs[0], refs[1:]
    sol, change = refs[:2]
    items = items_of(plan, step - 1, got, meta)
    changes = []
    for p in range(plan.quarter):
        j = table[plan.order + step % COLORS * plan.quarter + p]
        value = subtract(plan, resid[j], j.astype(jnp.float32), items)
        new = dot(value.astype(jnp.bfloat16), diag[j])
        sol[p] = new
        if has_old:
            new = new - old[p]
        changes.append(new.astype(jnp.bfloat16))
        change[p] = changes[p]
    products(plan, step, table, changes, coupling, refs[2:])


def forward_kernel(plan, step, phase, *refs):
    got, out = refs[1:-1], refs[-1]
    for s in plan.carried[phase]:
        lower = s & ((1 << phase) - 1)
        if lower:
            d = lower.bit_length() - 1
            length = plan.stride(step)
            out[pl.ds(plan.at(s, phase, step), length), :] = got[d][
                pl.ds(plan.at(s, d, step), length), :
            ]


def local_kernel(plan, step, last, table, resid, coupling, change, *refs):
    items = []
    if step > 0:
        items = items_of(plan, step - 1, refs[: plan.lanes], refs[plan.lanes : 2 * plan.lanes])
        refs = refs[2 * plan.lanes :]
    if last:
        sols, refs = refs[:COLORS], refs[COLORS:]
    out = refs[0]
    for r in range(plan.rows):
        out[r] = subtract(plan, resid[r], jnp.float32(r), items)
    for p in range(plan.quarter):
        at = step % COLORS * plan.quarter + p
        j = table[plan.order + at]
        both = dot(change[p], jnp.concatenate([coupling[j, 0], coupling[j, 1]], axis=1))
        for k in range(2):
            t = table[plan.local + 2 * at + k]
            out[t] = out[t] - both[:, k * plan.w : (k + 1) * plan.w]
    if last:
        for c in range(COLORS):
            for p in range(plan.quarter):
                refs[1][table[plan.order + c * plan.quarter + p]] = sols[c][p]


def final_kernel(plan, step, resid, *refs):
    items = items_of(plan, step, refs[: plan.lanes], refs[plan.lanes : 2 * plan.lanes])
    out = refs[-1]
    for r in range(plan.rows):
        out[r] = subtract(plan, resid[r], jnp.float32(r), items)


def on_device(coupling, diag_inv, rhs, color, local_target, group_peer, group_list, dom_target):
    rows, rhs_count, width = rhs.shape
    doms, group = lax.axis_size("dom"), lax.axis_size("sub")
    assert group & (group - 1) == 0 and doms % 2 == 0
    plan = Plan(rows, rhs_count, width, group)
    f32 = jnp.float32
    near_pairs = [(i, i ^ 1) for i in range(doms)]
    far_pairs = [(i, (i + 1 if i % 2 else i - 1) % doms) for i in range(doms)]
    params = pltpu.CompilerParams(vmem_limit_bytes=16 * 1024 * 1024)

    def call(body, name, ins, in_specs, outs, **kw):
        smem = [getattr(o, "memory_space", None) == pltpu.SMEM for o in outs]
        return pl.pallas_call(
            body,
            name=name,
            in_specs=in_specs + [VMEM] * (len(ins) - len(in_specs)),
            out_specs=[SMEM if s else VMEM for s in smem],
            out_shape=outs,
            compiler_params=params,
            **kw,
        )(*ins)

    def exchange(step, sends):
        got = [None] * plan.lanes
        arrived = []
        for d in range(plan.phases):
            send = sends[2 + d]
            if d:
                (send,) = call(
                    functools.partial(forward_kernel, plan, step, d),
                    f"forward{step}",
                    [send, *arrived],
                    [VMEM],
                    [plan.types(step)[2 + d]],
                    input_output_aliases={0: 0},
                )
            arrived.append(lax.ppermute(send, "sub", [(i, i ^ (1 << d)) for i in range(group)]))
            if d == 0:
                got[0] = lax.ppermute(sends[0], "dom", far_pairs)
        got[1] = lax.ppermute(sends[1], "dom", near_pairs)
        got[2:] = arrived
        return got

    sol_t = pltpu.VMEM((plan.quarter, plan.n, plan.w), f32)
    change_t = pltpu.VMEM((plan.quarter, plan.n, plan.w), jnp.bfloat16)
    resid_t = pltpu.VMEM(rhs.shape, f32)
    tables = [color, group_peer.T, group_list, dom_target.T, local_target.T]
    hbm = [pltpu.with_memory_space_constraint(a, pltpu.HBM) for a in tables + [rhs, diag_inv, coupling]]
    table_scratch = [tables[i].shape for i in (0, 4, 1, 2, 3)]
    table, tiles, diags, resid, sol, change, *sends = call(
        functools.partial(first_kernel, plan),
        "first",
        hbm,
        [HBM] * len(hbm),
        [
            pltpu.SMEM((plan.table,), jnp.int32),
            pltpu.VMEM(coupling.shape, coupling.dtype),
            pltpu.VMEM(diag_inv.shape, diag_inv.dtype),
            resid_t,
            sol_t,
            change_t,
        ]
        + plan.types(0),
        scratch_shapes=[pltpu.SMEM(shape, jnp.int32) for shape in table_scratch]
        + [pltpu.SemaphoreType.DMA((len(hbm),))],
    )
    sols = [sol]
    got = meta = None
    steps = SWEEPS * COLORS
    for step in range(steps):
        c = step % COLORS
        if step > 0:
            ins = [table, resid, diags, tiles, *got, *meta]
            if step >= COLORS:
                ins.append(sols[c])
            sol, change, *sends = call(
                functools.partial(step_kernel, plan, step),
                f"step{step}",
                ins,
                [SMEM],
                [sol_t, change_t] + plan.types(step),
            )
            sols[c:] = [sol] + sols[c + 1 :]
        last = step == steps - 1
        ins = [table, resid, tiles, change]
        if step > 0:
            ins += [*got, *meta]
        if last:
            ins += sols
        resid, *rest = call(
            functools.partial(local_kernel, plan, step, last),
            f"local{step}",
            ins,
            [SMEM],
            [resid_t] + ([jax.ShapeDtypeStruct(rhs.shape, f32)] if last else []),
            input_output_aliases={1: 0},
        )
        got = exchange(step, sends)
        if step == 0:
            meta = got
    (defect,) = call(
        functools.partial(final_kernel, plan, steps - 1),
        "final",
        [resid, *got, *meta],
        [],
        [jax.ShapeDtypeStruct(rhs.shape, f32)],
    )
    return rest[0], defect


def solution(mesh):
    placed = (
        P(("dom", "sub"), None, None, None),
        P(("dom", "sub"), None, None),
        P(("dom", "sub"), None, None),
        P(("dom", "sub")),
        P(("dom", "sub"), None),
        P(("dom", "sub"), None),
        P(("dom", "sub"), None, None),
        P(("dom", "sub"), None),
    )
    return jax.shard_map(
        on_device,
        mesh=mesh,
        in_specs=placed,
        out_specs=(P(("dom", "sub"), None, None), P(("dom", "sub"), None, None)),
        check_vma=False,
    )
```

```python
import functools

import jax
import jax.numpy as jnp
from jax import lax
from jax.experimental import pallas as pl
from jax.experimental.pallas import tpu as pltpu
from jax.sharding import PartitionSpec as P

COLORS = 4
SWEEPS = 2
META = 8

VMEM = pl.BlockSpec(memory_space=pltpu.VMEM)
SMEM = pl.BlockSpec(memory_space=pltpu.SMEM)
HBM = pl.BlockSpec(memory_space=pltpu.HBM)


def dot(a, b):
    return jnp.dot(a, b, preferred_element_type=jnp.float32)


class Plan:
    def __init__(self, rows, rhs_count, width, group):
        self.rows, self.n, self.w, self.group = rows, rhs_count, width, group
        self.quarter = rows // COLORS
        self.lanes = 3
        self.order, self.local, self.slot = 0, rows, 3 * rows
        self.table = 5 * rows
        self.dom_meta = -(-rows // 8) * 8

    def stride(self, step):
        return self.n + (META if step == 0 else 0)

    def at(self, member, step):
        return member * self.stride(step)

    def types(self, step):
        dom = self.quarter * self.n + (self.dom_meta if step == 0 else 0)
        shapes = [dom, dom] + [self.group * self.stride(step)]
        return [pltpu.VMEM((length, self.w), jnp.float32) for length in shapes]


def items_of(plan, step, got, meta):
    color = step % COLORS
    out = []
    for q in range(plan.group):
        out.append((meta[2], plan.at(q, 0) + plan.n + color, got[2], plan.at(q, step)))
    for lane in range(2):
        for p in range(plan.quarter):
            line = plan.quarter * plan.n + color * plan.quarter + p
            out.append((meta[lane], line, got[lane], p * plan.n))
    return out


def subtract(plan, value, row, items):
    for meta, line, got, start in items:
        here = meta[pl.ds(line, 1), :] == row
        value = value - jnp.where(here, got[pl.ds(start, plan.n), :], 0.0)
    return value


def products(plan, step, table, changes, coupling, sends):
    parity = lax.rem(lax.axis_index("dom"), 2)
    far, near = sends[:2]
    terms = []
    for p in range(plan.quarter):
        at = step % COLORS * plan.quarter + p
        j = table[plan.order + at]
        both = dot(changes[p], jnp.concatenate([coupling[j, 2], coupling[j, 3]], axis=1))
        for k in range(2):
            terms.append((table[plan.slot + 2 * at + k], both[:, k * plan.w : (k + 1) * plan.w]))
        both = dot(
            changes[p],
            jnp.concatenate([coupling[j, 5 - parity], coupling[j, 4 + parity]], axis=1),
        )
        far[pl.ds(p * plan.n, plan.n), :] = both[:, : plan.w]
        near[pl.ds(p * plan.n, plan.n), :] = both[:, plan.w :]
    for q in range(plan.group):
        total = jnp.zeros((plan.n, plan.w), jnp.float32)
        for slot, term in terms:
            total = total + jnp.where(slot == q, term, 0.0)
        sends[2][pl.ds(plan.at(q, step), plan.n), :] = total


def first_kernel(plan, *refs):
    hbm, outs, scratch = refs[:8], refs[8 : 14 + plan.lanes], refs[14 + plan.lanes :]
    table, coupling, diag, rhs, sol, change = outs[:6]
    sends = outs[6:]
    color, local_target, group_peer, group_list, dom_target = scratch[:5]
    sems = scratch[5]
    targets = (color, group_peer, group_list, dom_target, local_target, rhs, diag, coupling)
    copies = [
        pltpu.make_async_copy(src, dst, sems.at[i]) for i, (src, dst) in enumerate(zip(hbm, targets))
    ]
    for copy in copies:
        copy.start()
    for copy in copies[:5]:
        copy.wait()
    parity = lax.rem(lax.axis_index("dom"), 2)
    colors = [color[i] for i in range(plan.rows)]
    for i in range(plan.rows):
        before = jnp.int32(0)
        for e in range(i):
            before = before + (colors[e] == colors[i]).astype(jnp.int32)
        at = colors[i] * plan.quarter + before
        table[plan.order + at] = i
        for k in range(2):
            table[plan.local + 2 * at + k] = local_target[k, i]
            table[plan.slot + 2 * at + k] = group_peer[k, i]
    line = lax.broadcasted_iota(jnp.int32, (META, plan.w), 0)
    for q in range(plan.group):
        meta = jnp.full((META, plan.w), -1, jnp.int32)
        for c in range(COLORS):
            meta = jnp.where(line == c, group_list[0, c, q], meta)
        sends[2][pl.ds(plan.at(q, 0) + plan.n, META), :] = meta.astype(jnp.float32)
    line = lax.broadcasted_iota(jnp.int32, (plan.dom_meta, plan.w), 0)
    for send, k in zip(sends[:2], (1 - parity, parity)):
        meta = jnp.full((plan.dom_meta, plan.w), -1, jnp.int32)
        for at in range(plan.rows):
            meta = jnp.where(line == at, dom_target[k, table[plan.order + at]], meta)
        send[pl.ds(plan.quarter * plan.n, plan.dom_meta), :] = meta.astype(jnp.float32)
    copies[5].wait()
    copies[6].wait()
    changes = []
    for p in range(plan.quarter):
        j = table[plan.order + p]
        new = dot(rhs[j].astype(jnp.bfloat16), diag[j])
        sol[p] = new
        changes.append(new.astype(jnp.bfloat16))
        change[p] = changes[p]
    copies[7].wait()
    products(plan, 0, table, changes, coupling, sends)


def step_kernel(plan, step, table, resid, diag, coupling, *refs):
    got, meta, refs = refs[: plan.lanes], refs[plan.lanes : 2 * plan.lanes], refs[2 * plan.lanes :]
    has_old = step >= COLORS
    if has_old:
        old, refs = refs[0], refs[1:]
    sol, change = refs[:2]
    items = items_of(plan, step - 1, got, meta)
    changes = []
    for p in range(plan.quarter):
        j = table[plan.order + step % COLORS * plan.quarter + p]
        value = subtract(plan, resid[j], j.astype(jnp.float32), items)
        new = dot(value.astype(jnp.bfloat16), diag[j])
        sol[p] = new
        if has_old:
            new = new - old[p]
        changes.append(new.astype(jnp.bfloat16))
        change[p] = changes[p]
    products(plan, step, table, changes, coupling, refs[2:])


def local_kernel(plan, step, last, table, resid, coupling, change, *refs):
    items = []
    if step > 0:
        items = items_of(plan, step - 1, refs[: plan.lanes], refs[plan.lanes : 2 * plan.lanes])
        refs = refs[2 * plan.lanes :]
    if last:
        sols, refs = refs[:COLORS], refs[COLORS:]
    out = refs[0]
    for r in range(plan.rows):
        out[r] = subtract(plan, resid[r], jnp.float32(r), items)
    for p in range(plan.quarter):
        at = step % COLORS * plan.quarter + p
        j = table[plan.order + at]
        both = dot(change[p], jnp.concatenate([coupling[j, 0], coupling[j, 1]], axis=1))
        for k in range(2):
            t = table[plan.local + 2 * at + k]
            out[t] = out[t] - both[:, k * plan.w : (k + 1) * plan.w]
    if last:
        for c in range(COLORS):
            for p in range(plan.quarter):
                refs[1][table[plan.order + c * plan.quarter + p]] = sols[c][p]


def final_kernel(plan, step, resid, *refs):
    items = items_of(plan, step, refs[: plan.lanes], refs[plan.lanes : 2 * plan.lanes])
    out = refs[-1]
    for r in range(plan.rows):
        out[r] = subtract(plan, resid[r], jnp.float32(r), items)


def on_device(coupling, diag_inv, rhs, color, local_target, group_peer, group_list, dom_target):
    rows, rhs_count, width = rhs.shape
    doms, group = lax.axis_size("dom"), lax.axis_size("sub")
    assert doms % 2 == 0
    plan = Plan(rows, rhs_count, width, group)
    f32 = jnp.float32
    near_pairs = [(i, i ^ 1) for i in range(doms)]
    far_pairs = [(i, (i + 1 if i % 2 else i - 1) % doms) for i in range(doms)]
    params = pltpu.CompilerParams(vmem_limit_bytes=16 * 1024 * 1024)

    def call(body, name, ins, in_specs, outs, **kw):
        smem = [getattr(o, "memory_space", None) == pltpu.SMEM for o in outs]
        return pl.pallas_call(
            body,
            name=name,
            in_specs=in_specs + [VMEM] * (len(ins) - len(in_specs)),
            out_specs=[SMEM if s else VMEM for s in smem],
            out_shape=outs,
            compiler_params=params,
            **kw,
        )(*ins)

    def exchange(step, sends):
        far = lax.ppermute(sends[0], "dom", far_pairs)
        near = lax.ppermute(sends[1], "dom", near_pairs)
        return [far, near, lax.all_to_all(sends[2], "sub", 0, 0, tiled=True)]

    sol_t = pltpu.VMEM((plan.quarter, plan.n, plan.w), f32)
    change_t = pltpu.VMEM((plan.quarter, plan.n, plan.w), jnp.bfloat16)
    resid_t = pltpu.VMEM(rhs.shape, f32)
    tables = [color, group_peer.T, group_list, dom_target.T, local_target.T]
    hbm = [pltpu.with_memory_space_constraint(a, pltpu.HBM) for a in tables + [rhs, diag_inv, coupling]]
    table_scratch = [tables[i].shape for i in (0, 4, 1, 2, 3)]
    table, tiles, diags, resid, sol, change, *sends = call(
        functools.partial(first_kernel, plan),
        "first",
        hbm,
        [HBM] * len(hbm),
        [
            pltpu.SMEM((plan.table,), jnp.int32),
            pltpu.VMEM(coupling.shape, coupling.dtype),
            pltpu.VMEM(diag_inv.shape, diag_inv.dtype),
            resid_t,
            sol_t,
            change_t,
        ]
        + plan.types(0),
        scratch_shapes=[pltpu.SMEM(shape, jnp.int32) for shape in table_scratch]
        + [pltpu.SemaphoreType.DMA((len(hbm),))],
    )
    sols = [sol]
    got = meta = None
    steps = SWEEPS * COLORS
    for step in range(steps):
        c = step % COLORS
        if step > 0:
            ins = [table, resid, diags, tiles, *got, *meta]
            if step >= COLORS:
                ins.append(sols[c])
            sol, change, *sends = call(
                functools.partial(step_kernel, plan, step),
                f"step{step}",
                ins,
                [SMEM],
                [sol_t, change_t] + plan.types(step),
            )
            sols[c:] = [sol] + sols[c + 1 :]
        last = step == steps - 1
        ins = [table, resid, tiles, change]
        if step > 0:
            ins += [*got, *meta]
        if last:
            ins += sols
        resid, *rest = call(
            functools.partial(local_kernel, plan, step, last),
            f"local{step}",
            ins,
            [SMEM],
            [resid_t] + ([jax.ShapeDtypeStruct(rhs.shape, f32)] if last else []),
            input_output_aliases={1: 0},
        )
        got = exchange(step, sends)
        if step == 0:
            meta = got
    (defect,) = call(
        functools.partial(final_kernel, plan, steps - 1),
        "final",
        [resid, *got, *meta],
        [],
        [jax.ShapeDtypeStruct(rhs.shape, f32)],
    )
    return rest[0], defect


def solution(mesh):
    placed = (
        P(("dom", "sub"), None, None, None),
        P(("dom", "sub"), None, None),
        P(("dom", "sub"), None, None),
        P(("dom", "sub")),
        P(("dom", "sub"), None),
        P(("dom", "sub"), None),
        P(("dom", "sub"), None, None),
        P(("dom", "sub"), None),
    )
    return jax.shard_map(
        on_device,
        mesh=mesh,
        in_specs=placed,
        out_specs=(P(("dom", "sub"), None, None), P(("dom", "sub"), None, None)),
        check_vma=False,
    )
```

```python
import functools

import jax
import jax.numpy as jnp
from jax import lax
from jax.experimental import pallas as pl
from jax.experimental.pallas import tpu as pltpu
from jax.sharding import PartitionSpec as P

COLORS = 4
SWEEPS = 2
META = 8

VMEM = pl.BlockSpec(memory_space=pltpu.VMEM)
SMEM = pl.BlockSpec(memory_space=pltpu.SMEM)
HBM = pl.BlockSpec(memory_space=pltpu.HBM)


def dot(a, b):
    return jnp.dot(a, b, preferred_element_type=jnp.float32)


class Plan:
    def __init__(self, rows, rhs_count, width, group):
        self.rows, self.n, self.w, self.group = rows, rhs_count, width, group
        self.quarter = rows // COLORS
        self.phases = group.bit_length() - 1
        self.lanes = 2 + self.phases
        self.carried = [[s for s in range(1, group) if s >> d & 1] for d in range(self.phases)]
        self.order, self.local, self.slot = 0, rows, 3 * rows
        self.table = 5 * rows
        self.dom_meta = -(-rows // 8) * 8

    def turned(self, distance, back=False):
        half = self.phases // 2
        if back:
            half = self.phases - half
        return (distance >> half | distance << (self.phases - half)) & (self.group - 1)

    def stride(self, step):
        return self.n + (META if step == 0 else 0)

    def at(self, s, phase, step):
        return self.carried[phase].index(s) * self.stride(step)

    def types(self, step):
        dom = self.quarter * self.n + (self.dom_meta if step == 0 else 0)
        shapes = [dom, dom] + [len(c) * self.stride(step) for c in self.carried]
        return [pltpu.VMEM((length, self.w), jnp.float32) for length in shapes]


def items_of(plan, step, got, meta):
    color = step % COLORS
    out = []
    for s in range(1, plan.group):
        d = s.bit_length() - 1
        line = plan.at(s, d, 0) + plan.n + color
        out.append((meta[2 + d], line, got[2 + d], plan.at(s, d, step)))
    for lane in range(2):
        for p in range(plan.quarter):
            line = plan.quarter * plan.n + color * plan.quarter + p
            out.append((meta[lane], line, got[lane], p * plan.n))
    return out


def subtract(plan, value, row, items):
    for meta, line, got, start in items:
        here = meta[pl.ds(line, 1), :] == row
        value = value - jnp.where(here, got[pl.ds(start, plan.n), :], 0.0)
    return value


def products(plan, step, table, changes, coupling, sends):
    parity = lax.rem(lax.axis_index("dom"), 2)
    far, near = sends[:2]
    terms = []
    for p in range(plan.quarter):
        at = step % COLORS * plan.quarter + p
        j = table[plan.order + at]
        both = dot(changes[p], jnp.concatenate([coupling[j, 2], coupling[j, 3]], axis=1))
        for k in range(2):
            terms.append((table[plan.slot + 2 * at + k], both[:, k * plan.w : (k + 1) * plan.w]))
        both = dot(
            changes[p],
            jnp.concatenate([coupling[j, 5 - parity], coupling[j, 4 + parity]], axis=1),
        )
        far[pl.ds(p * plan.n, plan.n), :] = both[:, : plan.w]
        near[pl.ds(p * plan.n, plan.n), :] = both[:, plan.w :]
    for s in range(1, plan.group):
        total = jnp.zeros((plan.n, plan.w), jnp.float32)
        for slot, term in terms:
            total = total + jnp.where(slot == s, term, 0.0)
        d = (s & -s).bit_length() - 1
        sends[2 + d][pl.ds(plan.at(s, d, step), plan.n), :] = total


def first_kernel(plan, *refs):
    hbm, outs, scratch = refs[:8], refs[8 : 14 + plan.lanes], refs[14 + plan.lanes :]
    table, coupling, diag, rhs, sol, change = outs[:6]
    sends = outs[6:]
    color, local_target, group_peer, group_list, dom_target = scratch[:5]
    sems = scratch[5]
    targets = (color, group_peer, group_list, dom_target, local_target, rhs, diag, coupling)
    copies = [
        pltpu.make_async_copy(src, dst, sems.at[i]) for i, (src, dst) in enumerate(zip(hbm, targets))
    ]
    for copy in copies:
        copy.start()
    for copy in copies[:5]:
        copy.wait()
    me = lax.axis_index("sub")
    parity = lax.rem(lax.axis_index("dom"), 2)
    odd = parity == 1
    colors = [color[i] for i in range(plan.rows)]
    for i in range(plan.rows):
        before = jnp.int32(0)
        for e in range(i):
            before = before + (colors[e] == colors[i]).astype(jnp.int32)
        at = colors[i] * plan.quarter + before
        table[plan.order + at] = i
        for k in range(2):
            table[plan.local + 2 * at + k] = local_target[k, i]
            distance = me ^ group_peer[k, i]
            table[plan.slot + 2 * at + k] = jnp.where(odd, plan.turned(distance), distance)
    line = lax.broadcasted_iota(jnp.int32, (META, plan.w), 0)
    for s in range(1, plan.group):
        meta = jnp.full((META, plan.w), -1, jnp.int32)
        q = me ^ jnp.where(odd, plan.turned(s, back=True), s)
        for c in range(COLORS):
            meta = jnp.where(line == c, group_list[0, c, q], meta)
        d = (s & -s).bit_length() - 1
        sends[2 + d][pl.ds(plan.at(s, d, 0) + plan.n, META), :] = meta.astype(jnp.float32)
    line = lax.broadcasted_iota(jnp.int32, (plan.dom_meta, plan.w), 0)
    for send, k in zip(sends[:2], (1 - parity, parity)):
        meta = jnp.full((plan.dom_meta, plan.w), -1, jnp.int32)
        for at in range(plan.rows):
            meta = jnp.where(line == at, dom_target[k, table[plan.order + at]], meta)
        send[pl.ds(plan.quarter * plan.n, plan.dom_meta), :] = meta.astype(jnp.float32)
    copies[5].wait()
    copies[6].wait()
    changes = []
    for p in range(plan.quarter):
        j = table[plan.order + p]
        new = dot(rhs[j].astype(jnp.bfloat16), diag[j])
        sol[p] = new
        changes.append(new.astype(jnp.bfloat16))
        change[p] = changes[p]
    copies[7].wait()
    products(plan, 0, table, changes, coupling, sends)


def step_kernel(plan, step, table, resid, diag, coupling, *refs):
    got, meta, refs = refs[: plan.lanes], refs[plan.lanes : 2 * plan.lanes], refs[2 * plan.lanes :]
    has_old = step >= COLORS
    if has_old:
        old, refs = refs[0], refs[1:]
    sol, change = refs[:2]
    items = items_of(plan, step - 1, got, meta)
    changes = []
    for p in range(plan.quarter):
        j = table[plan.order + step % COLORS * plan.quarter + p]
        value = subtract(plan, resid[j], j.astype(jnp.float32), items)
        new = dot(value.astype(jnp.bfloat16), diag[j])
        sol[p] = new
        if has_old:
            new = new - old[p]
        changes.append(new.astype(jnp.bfloat16))
        change[p] = changes[p]
    products(plan, step, table, changes, coupling, refs[2:])


def forward_kernel(plan, step, phase, *refs):
    got, out = refs[2:-2], refs[-2]
    for s in plan.carried[phase]:
        lower = s & ((1 << phase) - 1)
        if lower:
            d = lower.bit_length() - 1
            length = plan.stride(step)
            out[pl.ds(plan.at(s, phase, step), length), :] = got[d][
                pl.ds(plan.at(s, d, step), length), :
            ]


def local_kernel(plan, step, last, table, resid, coupling, change, *refs):
    items = []
    if step > 0:
        items = items_of(plan, step - 1, refs[: plan.lanes], refs[plan.lanes : 2 * plan.lanes])
        refs = refs[2 * plan.lanes :]
    if last:
        sols, refs = refs[:COLORS], refs[COLORS:]
    out = refs[0]
    for r in range(plan.rows):
        out[r] = subtract(plan, resid[r], jnp.float32(r), items)
    for p in range(plan.quarter):
        at = step % COLORS * plan.quarter + p
        j = table[plan.order + at]
        both = dot(change[p], jnp.concatenate([coupling[j, 0], coupling[j, 1]], axis=1))
        for k in range(2):
            t = table[plan.local + 2 * at + k]
            out[t] = out[t] - both[:, k * plan.w : (k + 1) * plan.w]
    if last:
        for c in range(COLORS):
            for p in range(plan.quarter):
                refs[1][table[plan.order + c * plan.quarter + p]] = sols[c][p]


def final_kernel(plan, step, resid, *refs):
    items = items_of(plan, step, refs[: plan.lanes], refs[plan.lanes : 2 * plan.lanes])
    out = refs[-1]
    for r in range(plan.rows):
        out[r] = subtract(plan, resid[r], jnp.float32(r), items)


def on_device(coupling, diag_inv, rhs, color, local_target, group_peer, group_list, dom_target):
    rows, rhs_count, width = rhs.shape
    doms, group = lax.axis_size("dom"), lax.axis_size("sub")
    assert group & (group - 1) == 0 and doms % 2 == 0
    plan = Plan(rows, rhs_count, width, group)
    f32 = jnp.float32
    near_pairs = [(i, i ^ 1) for i in range(doms)]
    far_pairs = [(i, (i + 1 if i % 2 else i - 1) % doms) for i in range(doms)]
    flips = [(1 << d, plan.turned(1 << d, back=True)) for d in range(plan.phases)]
    group_pairs = [
        [(i * group + m, i * group + (m ^ flip[i % 2])) for i in range(doms) for m in range(group)]
        for flip in flips
    ]
    params = pltpu.CompilerParams(vmem_limit_bytes=16 * 1024 * 1024)

    def call(body, name, ins, in_specs, outs, **kw):
        smem = [getattr(o, "memory_space", None) == pltpu.SMEM for o in outs]
        return pl.pallas_call(
            body,
            name=name,
            in_specs=in_specs + [VMEM] * (len(ins) - len(in_specs)),
            out_specs=[SMEM if s else VMEM for s in smem],
            out_shape=outs,
            compiler_params=params,
            **kw,
        )(*ins)

    def exchange(step, sends):
        got = [None] * plan.lanes
        near = sends[1]
        arrived = []
        for d in range(plan.phases):
            send = sends[2 + d]
            if d:
                send, near = call(
                    functools.partial(forward_kernel, plan, step, d),
                    f"forward{step}",
                    [send, near, *arrived],
                    [],
                    [plan.types(step)[2 + d], plan.types(step)[1]],
                    input_output_aliases={0: 0, 1: 1},
                )
            arrived.append(lax.ppermute(send, ("dom", "sub"), group_pairs[d]))
            if d == 0:
                got[0] = lax.ppermute(sends[0], "dom", far_pairs)
        got[1] = lax.ppermute(near, "dom", near_pairs)
        got[2:] = arrived
        return got

    sol_t = pltpu.VMEM((plan.quarter, plan.n, plan.w), f32)
    change_t = pltpu.VMEM((plan.quarter, plan.n, plan.w), jnp.bfloat16)
    resid_t = pltpu.VMEM(rhs.shape, f32)
    tables = [color, group_peer.T, group_list, dom_target.T, local_target.T]
    hbm = [pltpu.with_memory_space_constraint(a, pltpu.HBM) for a in tables + [rhs, diag_inv, coupling]]
    table_scratch = [tables[i].shape for i in (0, 4, 1, 2, 3)]
    table, tiles, diags, resid, sol, change, *sends = call(
        functools.partial(first_kernel, plan),
        "first",
        hbm,
        [HBM] * len(hbm),
        [
            pltpu.SMEM((plan.table,), jnp.int32),
            pltpu.VMEM(coupling.shape, coupling.dtype),
            pltpu.VMEM(diag_inv.shape, diag_inv.dtype),
            resid_t,
            sol_t,
            change_t,
        ]
        + plan.types(0),
        scratch_shapes=[pltpu.SMEM(shape, jnp.int32) for shape in table_scratch]
        + [pltpu.SemaphoreType.DMA((len(hbm),))],
    )
    sols = [sol]
    got = meta = None
    steps = SWEEPS * COLORS
    for step in range(steps):
        c = step % COLORS
        if step > 0:
            ins = [table, resid, diags, tiles, *got, *meta]
            if step >= COLORS:
                ins.append(sols[c])
            sol, change, *sends = call(
                functools.partial(step_kernel, plan, step),
                f"step{step}",
                ins,
                [SMEM],
                [sol_t, change_t] + plan.types(step),
            )
            sols[c:] = [sol] + sols[c + 1 :]
        last = step == steps - 1
        ins = [table, resid, tiles, change]
        if step > 0:
            ins += [*got, *meta]
        if last:
            ins += sols
        resid, *rest = call(
            functools.partial(local_kernel, plan, step, last),
            f"local{step}",
            ins,
            [SMEM],
            [resid_t] + ([jax.ShapeDtypeStruct(rhs.shape, f32)] if last else []),
            input_output_aliases={1: 0},
        )
        got = exchange(step, sends)
        if step == 0:
            meta = got
    (defect,) = call(
        functools.partial(final_kernel, plan, steps - 1),
        "final",
        [resid, *got, *meta],
        [],
        [jax.ShapeDtypeStruct(rhs.shape, f32)],
    )
    return rest[0], defect


def solution(mesh):
    placed = (
        P(("dom", "sub"), None, None, None),
        P(("dom", "sub"), None, None),
        P(("dom", "sub"), None, None),
        P(("dom", "sub")),
        P(("dom", "sub"), None),
        P(("dom", "sub"), None),
        P(("dom", "sub"), None, None),
        P(("dom", "sub"), None),
    )
    return jax.shard_map(
        on_device,
        mesh=mesh,
        in_specs=placed,
        out_specs=(P(("dom", "sub"), None, None), P(("dom", "sub"), None, None)),
        check_vma=False,
    )
```

```python
import functools

import jax
import jax.numpy as jnp
from jax import lax
from jax.experimental import pallas as pl
from jax.experimental.pallas import tpu as pltpu
from jax.sharding import PartitionSpec as P

COLORS = 4
SWEEPS = 2
META = 8

VMEM = pl.BlockSpec(memory_space=pltpu.VMEM)
SMEM = pl.BlockSpec(memory_space=pltpu.SMEM)
HBM = pl.BlockSpec(memory_space=pltpu.HBM)


def dot(a, b):
    return jnp.dot(a, b, preferred_element_type=jnp.float32)


class Plan:
    def __init__(self, rows, rhs_count, width, group):
        self.rows, self.n, self.w, self.group = rows, rhs_count, width, group
        self.quarter = rows // COLORS
        self.lanes = group + 1
        self.order, self.local, self.slot = 0, rows, 3 * rows
        self.table = 5 * rows
        self.dom_meta = -(-rows // 8) * 8

    def types(self, step):
        extra = (self.dom_meta, META) if step == 0 else (0, 0)
        dom, one = self.quarter * self.n + extra[0], self.n + extra[1]
        shapes = [dom] + [one] * (self.group - 1) + [dom]
        return [pltpu.VMEM((length, self.w), jnp.float32) for length in shapes]


def items_of(plan, step, got, meta):
    color = step % COLORS
    out = []
    for lane in range(plan.lanes):
        if 0 < lane < plan.group:
            out.append((meta[lane], plan.n + color, got[lane], 0))
            continue
        for p in range(plan.quarter):
            line = plan.quarter * plan.n + color * plan.quarter + p
            out.append((meta[lane], line, got[lane], p * plan.n))
    return out


def subtract(plan, value, row, items):
    for meta, line, got, start in items:
        here = meta[pl.ds(line, 1), :] == row
        value = value - jnp.where(here, got[pl.ds(start, plan.n), :], 0.0)
    return value


def lanes_of(plan, refs):
    return refs[: plan.lanes], refs[plan.lanes :]


def products(plan, step, table, changes, coupling, sends):
    parity = lax.rem(lax.axis_index("dom"), 2)
    far, near = sends[0], sends[-1]
    terms = []
    for p in range(plan.quarter):
        at = step % COLORS * plan.quarter + p
        j = table[plan.order + at]
        both = dot(
            changes[p],
            jnp.concatenate([coupling[j, 5 - parity], coupling[j, 4 + parity]], axis=1),
        )
        far[pl.ds(p * plan.n, plan.n), :] = both[:, : plan.w]
        near[pl.ds(p * plan.n, plan.n), :] = both[:, plan.w :]
        both = dot(changes[p], jnp.concatenate([coupling[j, 2], coupling[j, 3]], axis=1))
        for k in range(2):
            terms.append((table[plan.slot + 2 * at + k], both[:, k * plan.w : (k + 1) * plan.w]))
    for s in range(1, plan.group):
        total = jnp.zeros((plan.n, plan.w), jnp.float32)
        for slot, term in terms:
            total = total + jnp.where(slot == s, term, 0.0)
        sends[s][pl.ds(0, plan.n), :] = total


def first_kernel(plan, *refs):
    hbm, outs, scratch = refs[:8], refs[8 : 14 + plan.lanes], refs[14 + plan.lanes :]
    table, coupling, diag, rhs, sol, change = outs[:6]
    sends = outs[6:]
    color, local_target, group_peer, group_list, dom_target = scratch[:5]
    sems = scratch[5]
    targets = (color, group_peer, group_list, dom_target, local_target, rhs, diag, coupling)
    copies = [
        pltpu.make_async_copy(src, dst, sems.at[i]) for i, (src, dst) in enumerate(zip(hbm, targets))
    ]
    for copy in copies:
        copy.start()
    for copy in copies[:5]:
        copy.wait()
    me = lax.axis_index("sub")
    parity = lax.rem(lax.axis_index("dom"), 2)
    colors = [color[i] for i in range(plan.rows)]
    for i in range(plan.rows):
        before = jnp.int32(0)
        for e in range(i):
            before = before + (colors[e] == colors[i]).astype(jnp.int32)
        at = colors[i] * plan.quarter + before
        table[plan.order + at] = i
        for k in range(2):
            table[plan.local + 2 * at + k] = local_target[k, i]
            table[plan.slot + 2 * at + k] = me ^ group_peer[k, i]
    line = lax.broadcasted_iota(jnp.int32, (META, plan.w), 0)
    for s in range(1, plan.group):
        meta = jnp.full((META, plan.w), -1, jnp.int32)
        for c in range(COLORS):
            meta = jnp.where(line == c, group_list[0, c, me ^ s], meta)
        sends[s][pl.ds(plan.n, META), :] = meta.astype(jnp.float32)
    line = lax.broadcasted_iota(jnp.int32, (plan.dom_meta, plan.w), 0)
    for send, k in ((sends[0], 1 - parity), (sends[-1], parity)):
        meta = jnp.full((plan.dom_meta, plan.w), -1, jnp.int32)
        for at in range(plan.rows):
            meta = jnp.where(line == at, dom_target[k, table[plan.order + at]], meta)
        send[pl.ds(plan.quarter * plan.n, plan.dom_meta), :] = meta.astype(jnp.float32)
    copies[5].wait()
    copies[6].wait()
    changes = []
    for p in range(plan.quarter):
        j = table[plan.order + p]
        new = dot(rhs[j].astype(jnp.bfloat16), diag[j])
        sol[p] = new
        changes.append(new.astype(jnp.bfloat16))
        change[p] = changes[p]
    copies[7].wait()
    products(plan, 0, table, changes, coupling, sends)


def step_kernel(plan, step, table, resid, diag, coupling, *refs):
    got, refs = lanes_of(plan, refs)
    meta, refs = lanes_of(plan, refs)
    has_old = step >= COLORS
    if has_old:
        old, refs = refs[0], refs[1:]
    sol, change = refs[:2]
    items = items_of(plan, step - 1, got, meta)
    changes = []
    for p in range(plan.quarter):
        j = table[plan.order + step % COLORS * plan.quarter + p]
        value = subtract(plan, resid[j], j.astype(jnp.float32), items)
        new = dot(value.astype(jnp.bfloat16), diag[j])
        sol[p] = new
        if has_old:
            new = new - old[p]
        changes.append(new.astype(jnp.bfloat16))
        change[p] = changes[p]
    products(plan, step, table, changes, coupling, refs[2:])


def local_kernel(plan, step, last, table, resid, coupling, change, near, *refs):
    items = []
    if step > 0:
        got, refs = lanes_of(plan, refs)
        meta, refs = lanes_of(plan, refs)
        items = items_of(plan, step - 1, got, meta)
    if last:
        sols, refs = refs[:COLORS], refs[COLORS:]
    out = refs[0]
    for r in range(plan.rows):
        out[r] = subtract(plan, resid[r], jnp.float32(r), items)
    for p in range(plan.quarter):
        at = step % COLORS * plan.quarter + p
        j = table[plan.order + at]
        both = dot(change[p], jnp.concatenate([coupling[j, 0], coupling[j, 1]], axis=1))
        for k in range(2):
            t = table[plan.local + 2 * at + k]
            out[t] = out[t] - both[:, k * plan.w : (k + 1) * plan.w]
    if last:
        for c in range(COLORS):
            for p in range(plan.quarter):
                refs[2][table[plan.order + c * plan.quarter + p]] = sols[c][p]


def final_kernel(plan, step, resid, *refs):
    got, refs = lanes_of(plan, refs)
    meta, refs = lanes_of(plan, refs)
    items = items_of(plan, step, got, meta)
    out = refs[-1]
    for r in range(plan.rows):
        out[r] = subtract(plan, resid[r], jnp.float32(r), items)


def on_device(coupling, diag_inv, rhs, color, local_target, group_peer, group_list, dom_target):
    rows, rhs_count, width = rhs.shape
    doms, group = lax.axis_size("dom"), lax.axis_size("sub")
    assert group & (group - 1) == 0 and doms % 2 == 0
    plan = Plan(rows, rhs_count, width, group)
    f32 = jnp.float32
    near_pairs = [(i, i ^ 1) for i in range(doms)]
    far_pairs = [(i, (i + 1 if i % 2 else i - 1) % doms) for i in range(doms)]
    params = pltpu.CompilerParams(vmem_limit_bytes=16 * 1024 * 1024)

    def call(body, name, ins, in_specs, outs, **kw):
        smem = [getattr(o, "memory_space", None) == pltpu.SMEM for o in outs]
        return pl.pallas_call(
            body,
            name=name,
            in_specs=in_specs + [VMEM] * (len(ins) - len(in_specs)),
            out_specs=[SMEM if s else VMEM for s in smem],
            out_shape=outs,
            compiler_params=params,
            **kw,
        )(*ins)

    def exchange(sends):
        got = [lax.ppermute(sends[0], "dom", far_pairs)]
        for s in reversed(range(1, group)):
            got.insert(1, lax.ppermute(sends[s], "sub", [(i, i ^ s) for i in range(group)]))
        return got + [lax.ppermute(sends[-1], "dom", near_pairs)]

    sol_t = pltpu.VMEM((plan.quarter, plan.n, plan.w), f32)
    change_t = pltpu.VMEM((plan.quarter, plan.n, plan.w), jnp.bfloat16)
    resid_t = pltpu.VMEM(rhs.shape, f32)
    tables = [color, group_peer.T, group_list, dom_target.T, local_target.T]
    hbm = [pltpu.with_memory_space_constraint(a, pltpu.HBM) for a in tables + [rhs, diag_inv, coupling]]
    table_scratch = [tables[i].shape for i in (0, 4, 1, 2, 3)]
    table, tiles, diags, resid, sol, change, *sends = call(
        functools.partial(first_kernel, plan),
        "first",
        hbm,
        [HBM] * len(hbm),
        [
            pltpu.SMEM((plan.table,), jnp.int32),
            pltpu.VMEM(coupling.shape, coupling.dtype),
            pltpu.VMEM(diag_inv.shape, diag_inv.dtype),
            resid_t,
            sol_t,
            change_t,
        ]
        + plan.types(0),
        scratch_shapes=[pltpu.SMEM(shape, jnp.int32) for shape in table_scratch]
        + [pltpu.SemaphoreType.DMA((len(hbm),))],
    )
    sols = [sol]
    got = meta = None
    steps = SWEEPS * COLORS
    for step in range(steps):
        c = step % COLORS
        if step > 0:
            ins = [table, resid, diags, tiles, *got, *meta]
            if step >= COLORS:
                ins.append(sols[c])
            sol, change, *sends = call(
                functools.partial(step_kernel, plan, step),
                f"step{step}",
                ins,
                [SMEM],
                [sol_t, change_t] + plan.types(step),
            )
            sols[c:] = [sol] + sols[c + 1 :]
        last = step == steps - 1
        ins = [table, resid, tiles, change, sends[-1]]
        if step > 0:
            ins += [*got, *meta]
        if last:
            ins += sols
        resid, sends[-1], *rest = call(
            functools.partial(local_kernel, plan, step, last),
            f"local{step}",
            ins,
            [SMEM],
            [resid_t, plan.types(step)[-1]] + ([jax.ShapeDtypeStruct(rhs.shape, f32)] if last else []),
            input_output_aliases={1: 0, 4: 1},
        )
        got = exchange(sends)
        if step == 0:
            meta = got
    (defect,) = call(
        functools.partial(final_kernel, plan, steps - 1),
        "final",
        [resid, *got, *meta],
        [],
        [jax.ShapeDtypeStruct(rhs.shape, f32)],
    )
    return rest[0], defect


def solution(mesh):
    placed = (
        P(("dom", "sub"), None, None, None),
        P(("dom", "sub"), None, None),
        P(("dom", "sub"), None, None),
        P(("dom", "sub")),
        P(("dom", "sub"), None),
        P(("dom", "sub"), None),
        P(("dom", "sub"), None, None),
        P(("dom", "sub"), None),
    )
    return jax.shard_map(
        on_device,
        mesh=mesh,
        in_specs=placed,
        out_specs=(P(("dom", "sub"), None, None), P(("dom", "sub"), None, None)),
        check_vma=False,
    )
```

```python
import functools

import jax
import jax.numpy as jnp
from jax import lax
from jax.experimental import pallas as pl
from jax.experimental.pallas import tpu as pltpu
from jax.sharding import PartitionSpec as P

COLORS = 4
SWEEPS = 2
META = 8

VMEM = pl.BlockSpec(memory_space=pltpu.VMEM)
SMEM = pl.BlockSpec(memory_space=pltpu.SMEM)
HBM = pl.BlockSpec(memory_space=pltpu.HBM)


def dot(a, b):
    return jnp.dot(a, b, preferred_element_type=jnp.float32)


class Plan:
    def __init__(self, rows, rhs_count, width, group):
        self.rows, self.n, self.w, self.group = rows, rhs_count, width, group
        self.quarter = rows // COLORS
        self.lanes = group + self.quarter
        self.distances = [1] + list(reversed(range(2, group)))
        self.order, self.local, self.slot = 0, rows, 3 * rows
        self.table = 5 * rows
        self.dom_meta = -(-rows // 8) * 8

    def types(self, step):
        extra = (self.dom_meta, META) if step == 0 else (0, 0)
        far, one = self.quarter * self.n + extra[0], self.n + extra[1]
        shapes = [far] + [one] * (self.lanes - 1)
        return [pltpu.VMEM((length, self.w), jnp.float32) for length in shapes]


def items_of(plan, step, got, meta):
    color = step % COLORS
    out = []
    for p in range(plan.quarter):
        line = plan.quarter * plan.n + color * plan.quarter + p
        out.append((meta[0], line, got[0], p * plan.n))
    for lane in range(1, plan.lanes):
        out.append((meta[lane], plan.n + color, got[lane], 0))
    return out


def subtract(plan, value, row, items):
    for meta, line, got, start in items:
        here = meta[pl.ds(line, 1), :] == row
        value = value - jnp.where(here, got[pl.ds(start, plan.n), :], 0.0)
    return value


def lanes_of(plan, refs):
    return refs[: plan.lanes], refs[plan.lanes :]


def products(plan, step, table, changes, coupling, sends):
    parity = lax.rem(lax.axis_index("dom"), 2)
    far, near = sends[0], sends[plan.group :]
    terms = []
    for p in range(plan.quarter):
        at = step % COLORS * plan.quarter + p
        j = table[plan.order + at]
        both = dot(
            changes[p],
            jnp.concatenate([coupling[j, 5 - parity], coupling[j, 4 + parity]], axis=1),
        )
        far[pl.ds(p * plan.n, plan.n), :] = both[:, : plan.w]
        near[p][pl.ds(0, plan.n), :] = both[:, plan.w :]
        both = dot(changes[p], jnp.concatenate([coupling[j, 2], coupling[j, 3]], axis=1))
        for k in range(2):
            terms.append((table[plan.slot + 2 * at + k], both[:, k * plan.w : (k + 1) * plan.w]))
    for lane, s in enumerate(plan.distances):
        total = jnp.zeros((plan.n, plan.w), jnp.float32)
        for slot, term in terms:
            total = total + jnp.where(slot == s, term, 0.0)
        sends[1 + lane][pl.ds(0, plan.n), :] = total


def first_kernel(plan, *refs):
    hbm, outs, scratch = refs[:8], refs[8 : 14 + plan.lanes], refs[14 + plan.lanes :]
    table, coupling, diag, rhs, sol, change = outs[:6]
    sends = outs[6:]
    color, local_target, group_peer, group_list, dom_target = scratch[:5]
    sems = scratch[5]
    targets = (color, group_peer, group_list, dom_target, local_target, rhs, diag, coupling)
    copies = [
        pltpu.make_async_copy(src, dst, sems.at[i]) for i, (src, dst) in enumerate(zip(hbm, targets))
    ]
    for copy in copies:
        copy.start()
    for copy in copies[:5]:
        copy.wait()
    me = lax.axis_index("sub")
    parity = lax.rem(lax.axis_index("dom"), 2)
    colors = [color[i] for i in range(plan.rows)]
    for i in range(plan.rows):
        before = jnp.int32(0)
        for e in range(i):
            before = before + (colors[e] == colors[i]).astype(jnp.int32)
        at = colors[i] * plan.quarter + before
        table[plan.order + at] = i
        for k in range(2):
            table[plan.local + 2 * at + k] = local_target[k, i]
            table[plan.slot + 2 * at + k] = me ^ group_peer[k, i]
    line = lax.broadcasted_iota(jnp.int32, (META, plan.w), 0)
    for lane, s in enumerate(plan.distances):
        meta = jnp.full((META, plan.w), -1, jnp.int32)
        for c in range(COLORS):
            meta = jnp.where(line == c, group_list[0, c, me ^ s], meta)
        sends[1 + lane][pl.ds(plan.n, META), :] = meta.astype(jnp.float32)
    for p in range(plan.quarter):
        meta = jnp.full((META, plan.w), -1, jnp.int32)
        for c in range(COLORS):
            at = c * plan.quarter + p
            meta = jnp.where(line == c, dom_target[parity, table[plan.order + at]], meta)
        sends[plan.group + p][pl.ds(plan.n, META), :] = meta.astype(jnp.float32)
    line = lax.broadcasted_iota(jnp.int32, (plan.dom_meta, plan.w), 0)
    meta = jnp.full((plan.dom_meta, plan.w), -1, jnp.int32)
    for at in range(plan.rows):
        meta = jnp.where(line == at, dom_target[1 - parity, table[plan.order + at]], meta)
    sends[0][pl.ds(plan.quarter * plan.n, plan.dom_meta), :] = meta.astype(jnp.float32)
    copies[5].wait()
    copies[6].wait()
    changes = []
    for p in range(plan.quarter):
        j = table[plan.order + p]
        new = dot(rhs[j].astype(jnp.bfloat16), diag[j])
        sol[p] = new
        changes.append(new.astype(jnp.bfloat16))
        change[p] = changes[p]
    copies[7].wait()
    products(plan, 0, table, changes, coupling, sends)


def step_kernel(plan, step, table, resid, diag, coupling, *refs):
    got, refs = lanes_of(plan, refs)
    meta, refs = lanes_of(plan, refs)
    has_old = step >= COLORS
    if has_old:
        old, refs = refs[0], refs[1:]
    sol, change = refs[:2]
    items = items_of(plan, step - 1, got, meta)
    changes = []
    for p in range(plan.quarter):
        j = table[plan.order + step % COLORS * plan.quarter + p]
        value = subtract(plan, resid[j], j.astype(jnp.float32), items)
        new = dot(value.astype(jnp.bfloat16), diag[j])
        sol[p] = new
        if has_old:
            new = new - old[p]
        changes.append(new.astype(jnp.bfloat16))
        change[p] = changes[p]
    products(plan, step, table, changes, coupling, refs[2:])


def local_kernel(plan, step, last, table, resid, coupling, change, *refs):
    items = []
    if step > 0:
        got, refs = lanes_of(plan, refs)
        meta, refs = lanes_of(plan, refs)
        items = items_of(plan, step - 1, got, meta)
    if last:
        sols, refs = refs[:COLORS], refs[COLORS:]
    out = refs[0]
    for r in range(plan.rows):
        out[r] = subtract(plan, resid[r], jnp.float32(r), items)
    for p in range(plan.quarter):
        at = step % COLORS * plan.quarter + p
        j = table[plan.order + at]
        both = dot(change[p], jnp.concatenate([coupling[j, 0], coupling[j, 1]], axis=1))
        for k in range(2):
            t = table[plan.local + 2 * at + k]
            out[t] = out[t] - both[:, k * plan.w : (k + 1) * plan.w]
    if last:
        for c in range(COLORS):
            for p in range(plan.quarter):
                refs[1][table[plan.order + c * plan.quarter + p]] = sols[c][p]


def final_kernel(plan, step, resid, *refs):
    got, refs = lanes_of(plan, refs)
    meta, refs = lanes_of(plan, refs)
    items = items_of(plan, step, got, meta)
    out = refs[-1]
    for r in range(plan.rows):
        out[r] = subtract(plan, resid[r], jnp.float32(r), items)


def on_device(coupling, diag_inv, rhs, color, local_target, group_peer, group_list, dom_target):
    rows, rhs_count, width = rhs.shape
    doms, group = lax.axis_size("dom"), lax.axis_size("sub")
    assert group & (group - 1) == 0 and doms % 2 == 0
    plan = Plan(rows, rhs_count, width, group)
    f32 = jnp.float32
    near_pairs = [(i, i ^ 1) for i in range(doms)]
    far_pairs = [(i, (i + 1 if i % 2 else i - 1) % doms) for i in range(doms)]
    params = pltpu.CompilerParams(vmem_limit_bytes=16 * 1024 * 1024)

    def call(body, name, ins, in_specs, outs, **kw):
        smem = [getattr(o, "memory_space", None) == pltpu.SMEM for o in outs]
        return pl.pallas_call(
            body,
            name=name,
            in_specs=in_specs + [VMEM] * (len(ins) - len(in_specs)),
            out_specs=[SMEM if s else VMEM for s in smem],
            out_shape=outs,
            compiler_params=params,
            **kw,
        )(*ins)

    def exchange(sends):
        got = [lax.ppermute(sends[0], "dom", far_pairs)]
        for send, s in zip(sends[1:group], plan.distances):
            got.append(lax.ppermute(send, "sub", [(i, i ^ s) for i in range(group)]))
        return got + [lax.ppermute(send, "dom", near_pairs) for send in sends[group:]]

    sol_t = pltpu.VMEM((plan.quarter, plan.n, plan.w), f32)
    change_t = pltpu.VMEM((plan.quarter, plan.n, plan.w), jnp.bfloat16)
    resid_t = pltpu.VMEM(rhs.shape, f32)
    tables = [color, group_peer.T, group_list, dom_target.T, local_target.T]
    hbm = [pltpu.with_memory_space_constraint(a, pltpu.HBM) for a in tables + [rhs, diag_inv, coupling]]
    table_scratch = [tables[i].shape for i in (0, 4, 1, 2, 3)]
    table, tiles, diags, resid, sol, change, *sends = call(
        functools.partial(first_kernel, plan),
        "first",
        hbm,
        [HBM] * len(hbm),
        [
            pltpu.SMEM((plan.table,), jnp.int32),
            pltpu.VMEM(coupling.shape, coupling.dtype),
            pltpu.VMEM(diag_inv.shape, diag_inv.dtype),
            resid_t,
            sol_t,
            change_t,
        ]
        + plan.types(0),
        scratch_shapes=[pltpu.SMEM(shape, jnp.int32) for shape in table_scratch]
        + [pltpu.SemaphoreType.DMA((len(hbm),))],
    )
    sols = [sol]
    got = meta = None
    steps = SWEEPS * COLORS
    for step in range(steps):
        c = step % COLORS
        if step > 0:
            ins = [table, resid, diags, tiles, *got, *meta]
            if step >= COLORS:
                ins.append(sols[c])
            sol, change, *sends = call(
                functools.partial(step_kernel, plan, step),
                f"step{step}",
                ins,
                [SMEM],
                [sol_t, change_t] + plan.types(step),
            )
            sols[c:] = [sol] + sols[c + 1 :]
        last = step == steps - 1
        ins = [table, resid, tiles, change]
        if step > 0:
            ins += [*got, *meta]
        if last:
            ins += sols
        resid, *rest = call(
            functools.partial(local_kernel, plan, step, last),
            f"local{step}",
            ins,
            [SMEM],
            [resid_t] + ([jax.ShapeDtypeStruct(rhs.shape, f32)] if last else []),
            input_output_aliases={1: 0},
        )
        got = exchange(sends)
        if step == 0:
            meta = got
    (defect,) = call(
        functools.partial(final_kernel, plan, steps - 1),
        "final",
        [resid, *got, *meta],
        [],
        [jax.ShapeDtypeStruct(rhs.shape, f32)],
    )
    return rest[0], defect


def solution(mesh):
    placed = (
        P(("dom", "sub"), None, None, None),
        P(("dom", "sub"), None, None),
        P(("dom", "sub"), None, None),
        P(("dom", "sub")),
        P(("dom", "sub"), None),
        P(("dom", "sub"), None),
        P(("dom", "sub"), None, None),
        P(("dom", "sub"), None),
    )
    return jax.shard_map(
        on_device,
        mesh=mesh,
        in_specs=placed,
        out_specs=(P(("dom", "sub"), None, None), P(("dom", "sub"), None, None)),
        check_vma=False,
    )
```

```python
import functools

import jax
import jax.numpy as jnp
from jax import lax
from jax.experimental import pallas as pl
from jax.experimental.pallas import tpu as pltpu
from jax.sharding import PartitionSpec as P

COLORS = 4
SWEEPS = 2
META = 8

VMEM = pl.BlockSpec(memory_space=pltpu.VMEM)
SMEM = pl.BlockSpec(memory_space=pltpu.SMEM)
HBM = pl.BlockSpec(memory_space=pltpu.HBM)


def dot(a, b):
    return jnp.dot(a, b, preferred_element_type=jnp.float32)


class Plan:
    def __init__(self, rows, rhs_count, width, group):
        self.rows, self.n, self.w, self.group = rows, rhs_count, width, group
        self.quarter = rows // COLORS
        self.lanes = group + self.quarter
        self.distances = [1] + list(reversed(range(2, group)))
        self.order, self.local, self.slot = 0, rows, 3 * rows
        self.table = 5 * rows
        self.dom_meta = -(-rows // 8) * 8

    def types(self, step):
        extra = (self.dom_meta, META) if step == 0 else (0, 0)
        far, one = self.quarter * self.n + extra[0], self.n + extra[1]
        shapes = [far] + [one] * (self.lanes - 1)
        return [pltpu.VMEM((length, self.w), jnp.float32) for length in shapes]


def items_of(plan, step, got, meta):
    color = step % COLORS
    out = []
    for p in range(plan.quarter):
        line = plan.quarter * plan.n + color * plan.quarter + p
        out.append((meta[0], line, got[0], p * plan.n))
    for lane in range(1, plan.lanes):
        out.append((meta[lane], plan.n + color, got[lane], 0))
    return out


def subtract(plan, value, row, items):
    for meta, line, got, start in items:
        here = meta[pl.ds(line, 1), :] == row
        value = value - jnp.where(here, got[pl.ds(start, plan.n), :], 0.0)
    return value


def lanes_of(plan, refs):
    return refs[: plan.lanes], refs[plan.lanes :]


def products(plan, step, table, changes, coupling, sends):
    parity = lax.rem(lax.axis_index("dom"), 2)
    far, near = sends[0], sends[plan.group :]
    terms = []
    for p in range(plan.quarter):
        at = step % COLORS * plan.quarter + p
        j = table[plan.order + at]
        both = dot(
            changes[p],
            jnp.concatenate([coupling[j, 5 - parity], coupling[j, 4 + parity]], axis=1),
        )
        far[pl.ds(p * plan.n, plan.n), :] = both[:, : plan.w]
        near[p][pl.ds(0, plan.n), :] = both[:, plan.w :]
        both = dot(changes[p], jnp.concatenate([coupling[j, 2], coupling[j, 3]], axis=1))
        for k in range(2):
            terms.append((table[plan.slot + 2 * at + k], both[:, k * plan.w : (k + 1) * plan.w]))
    for lane, s in enumerate(plan.distances):
        total = jnp.zeros((plan.n, plan.w), jnp.float32)
        for slot, term in terms:
            total = total + jnp.where(slot == s, term, 0.0)
        sends[1 + lane][pl.ds(0, plan.n), :] = total


def first_kernel(plan, *refs):
    hbm, outs, scratch = refs[:8], refs[8 : 14 + plan.lanes], refs[14 + plan.lanes :]
    table, coupling, diag, rhs, sol, change = outs[:6]
    sends = outs[6:]
    color, local_target, group_peer, group_list, dom_target = scratch[:5]
    sems = scratch[5]
    targets = (color, group_peer, group_list, dom_target, local_target, rhs, diag, coupling)
    copies = [
        pltpu.make_async_copy(src, dst, sems.at[i]) for i, (src, dst) in enumerate(zip(hbm, targets))
    ]
    for copy in copies:
        copy.start()
    for copy in copies[:5]:
        copy.wait()
    me = lax.axis_index("sub")
    parity = lax.rem(lax.axis_index("dom"), 2)
    colors = [color[i] for i in range(plan.rows)]
    for i in range(plan.rows):
        before = jnp.int32(0)
        for e in range(i):
            before = before + (colors[e] == colors[i]).astype(jnp.int32)
        at = colors[i] * plan.quarter + before
        table[plan.order + at] = i
        for k in range(2):
            table[plan.local + 2 * at + k] = local_target[k, i]
            table[plan.slot + 2 * at + k] = me ^ group_peer[k, i]
    copies[5].wait()
    copies[6].wait()
    changes = []
    for p in range(plan.quarter):
        j = table[plan.order + p]
        new = dot(rhs[j].astype(jnp.bfloat16), diag[j])
        sol[p] = new
        changes.append(new.astype(jnp.bfloat16))
        change[p] = changes[p]
    copies[7].wait()
    products(plan, 0, table, changes, coupling, sends)
    line = lax.broadcasted_iota(jnp.int32, (META, plan.w), 0)
    for lane, s in enumerate(plan.distances):
        meta = jnp.full((META, plan.w), -1, jnp.int32)
        for c in range(COLORS):
            meta = jnp.where(line == c, group_list[0, c, me ^ s], meta)
        sends[1 + lane][pl.ds(plan.n, META), :] = meta.astype(jnp.float32)
    for p in range(plan.quarter):
        meta = jnp.full((META, plan.w), -1, jnp.int32)
        for c in range(COLORS):
            at = c * plan.quarter + p
            meta = jnp.where(line == c, dom_target[parity, table[plan.order + at]], meta)
        sends[plan.group + p][pl.ds(plan.n, META), :] = meta.astype(jnp.float32)
    line = lax.broadcasted_iota(jnp.int32, (plan.dom_meta, plan.w), 0)
    meta = jnp.full((plan.dom_meta, plan.w), -1, jnp.int32)
    for at in range(plan.rows):
        meta = jnp.where(line == at, dom_target[1 - parity, table[plan.order + at]], meta)
    sends[0][pl.ds(plan.quarter * plan.n, plan.dom_meta), :] = meta.astype(jnp.float32)


def step_kernel(plan, step, table, resid, diag, coupling, *refs):
    got, refs = lanes_of(plan, refs)
    meta, refs = lanes_of(plan, refs)
    has_old = step >= COLORS
    if has_old:
        old, refs = refs[0], refs[1:]
    sol, change = refs[:2]
    items = items_of(plan, step - 1, got, meta)
    changes = []
    for p in range(plan.quarter):
        j = table[plan.order + step % COLORS * plan.quarter + p]
        value = subtract(plan, resid[j], j.astype(jnp.float32), items)
        new = dot(value.astype(jnp.bfloat16), diag[j])
        sol[p] = new
        if has_old:
            new = new - old[p]
        changes.append(new.astype(jnp.bfloat16))
        change[p] = changes[p]
    products(plan, step, table, changes, coupling, refs[2:])


def local_kernel(plan, step, last, table, resid, coupling, change, *refs):
    items = []
    if step > 0:
        got, refs = lanes_of(plan, refs)
        meta, refs = lanes_of(plan, refs)
        items = items_of(plan, step - 1, got, meta)
    if last:
        sols, refs = refs[:COLORS], refs[COLORS:]
    out = refs[0]
    for r in range(plan.rows):
        out[r] = subtract(plan, resid[r], jnp.float32(r), items)
    for p in range(plan.quarter):
        at = step % COLORS * plan.quarter + p
        j = table[plan.order + at]
        both = dot(change[p], jnp.concatenate([coupling[j, 0], coupling[j, 1]], axis=1))
        for k in range(2):
            t = table[plan.local + 2 * at + k]
            out[t] = out[t] - both[:, k * plan.w : (k + 1) * plan.w]
    if last:
        for c in range(COLORS):
            for p in range(plan.quarter):
                refs[1][table[plan.order + c * plan.quarter + p]] = sols[c][p]


def final_kernel(plan, step, resid, *refs):
    got, refs = lanes_of(plan, refs)
    meta, refs = lanes_of(plan, refs)
    items = items_of(plan, step, got, meta)
    out, rows, sems = refs
    copies = []
    for r in range(plan.rows):
        rows[r] = subtract(plan, resid[r], jnp.float32(r), items)
        copies.append(pltpu.make_async_copy(rows.at[r], out.at[r], sems.at[r]))
        copies[r].start()
    for copy in copies:
        copy.wait()


def on_device(coupling, diag_inv, rhs, color, local_target, group_peer, group_list, dom_target):
    rows, rhs_count, width = rhs.shape
    doms, group = lax.axis_size("dom"), lax.axis_size("sub")
    assert group & (group - 1) == 0 and doms % 2 == 0
    plan = Plan(rows, rhs_count, width, group)
    f32 = jnp.float32
    near_pairs = [(i, i ^ 1) for i in range(doms)]
    far_pairs = [(i, (i + 1 if i % 2 else i - 1) % doms) for i in range(doms)]
    params = pltpu.CompilerParams(vmem_limit_bytes=16 * 1024 * 1024)

    def call(body, name, ins, in_specs, outs, **kw):
        smem = [getattr(o, "memory_space", None) == pltpu.SMEM for o in outs]
        out_specs = kw.pop("out_specs", [SMEM if s else VMEM for s in smem])
        return pl.pallas_call(
            body,
            name=name,
            in_specs=in_specs + [VMEM] * (len(ins) - len(in_specs)),
            out_specs=out_specs,
            out_shape=outs,
            compiler_params=params,
            **kw,
        )(*ins)

    def exchange(sends):
        got = [lax.ppermute(sends[0], "dom", far_pairs)]
        for send, s in zip(sends[1:group], plan.distances):
            got.append(lax.ppermute(send, "sub", [(i, i ^ s) for i in range(group)]))
        return got + [lax.ppermute(send, "dom", near_pairs) for send in sends[group:]]

    sol_t = pltpu.VMEM((plan.quarter, plan.n, plan.w), f32)
    change_t = pltpu.VMEM((plan.quarter, plan.n, plan.w), jnp.bfloat16)
    resid_t = pltpu.VMEM(rhs.shape, f32)
    tables = [color, group_peer.T, group_list, dom_target.T, local_target.T]
    hbm = [pltpu.with_memory_space_constraint(a, pltpu.HBM) for a in tables + [rhs, diag_inv, coupling]]
    table_scratch = [tables[i].shape for i in (0, 4, 1, 2, 3)]
    table, tiles, diags, resid, sol, change, *sends = call(
        functools.partial(first_kernel, plan),
        "first",
        hbm,
        [HBM] * len(hbm),
        [
            pltpu.SMEM((plan.table,), jnp.int32),
            pltpu.VMEM(coupling.shape, coupling.dtype),
            pltpu.VMEM(diag_inv.shape, diag_inv.dtype),
            resid_t,
            sol_t,
            change_t,
        ]
        + plan.types(0),
        scratch_shapes=[pltpu.SMEM(shape, jnp.int32) for shape in table_scratch]
        + [pltpu.SemaphoreType.DMA((len(hbm),))],
    )
    sols = [sol]
    got = meta = None
    steps = SWEEPS * COLORS
    for step in range(steps):
        c = step % COLORS
        if step > 0:
            ins = [table, resid, diags, tiles, *got, *meta]
            if step >= COLORS:
                ins.append(sols[c])
            sol, change, *sends = call(
                functools.partial(step_kernel, plan, step),
                f"step{step}",
                ins,
                [SMEM],
                [sol_t, change_t] + plan.types(step),
            )
            sols[c:] = [sol] + sols[c + 1 :]
        last = step == steps - 1
        ins = [table, resid, tiles, change]
        if step > 0:
            ins += [*got, *meta]
        if last:
            ins += sols
        resid, *rest = call(
            functools.partial(local_kernel, plan, step, last),
            f"local{step}",
            ins,
            [SMEM],
            [resid_t] + ([jax.ShapeDtypeStruct(rhs.shape, f32)] if last else []),
            input_output_aliases={1: 0},
        )
        got = exchange(sends)
        if step == 0:
            meta = got
    (defect,) = call(
        functools.partial(final_kernel, plan, steps - 1),
        "final",
        [resid, *got, *meta],
        [],
        [jax.ShapeDtypeStruct(rhs.shape, f32)],
        out_specs=[HBM],
        scratch_shapes=[pltpu.VMEM(rhs.shape, f32), pltpu.SemaphoreType.DMA((rows,))],
    )
    return rest[0], defect


def solution(mesh):
    placed = (
        P(("dom", "sub"), None, None, None),
        P(("dom", "sub"), None, None),
        P(("dom", "sub"), None, None),
        P(("dom", "sub")),
        P(("dom", "sub"), None),
        P(("dom", "sub"), None),
        P(("dom", "sub"), None, None),
        P(("dom", "sub"), None),
    )
    return jax.shard_map(
        on_device,
        mesh=mesh,
        in_specs=placed,
        out_specs=(P(("dom", "sub"), None, None), P(("dom", "sub"), None, None)),
        check_vma=False,
    )
```

```python
import functools

import jax
import jax.numpy as jnp
from jax import lax
from jax.experimental import pallas as pl
from jax.experimental.pallas import tpu as pltpu
from jax.sharding import PartitionSpec as P

COLORS = 4
SWEEPS = 2
META = 8

VMEM = pl.BlockSpec(memory_space=pltpu.VMEM)
SMEM = pl.BlockSpec(memory_space=pltpu.SMEM)
HBM = pl.BlockSpec(memory_space=pltpu.HBM)


def dot(a, b):
    return jnp.dot(a, b, preferred_element_type=jnp.float32)


class Plan:
    def __init__(self, rows, rhs_count, width, group):
        self.rows, self.n, self.w, self.group = rows, rhs_count, width, group
        self.quarter = rows // COLORS
        self.lanes = group + self.quarter
        self.distances = [1] + list(reversed(range(2, group)))
        self.order, self.local, self.slot = 0, rows, 3 * rows
        self.table = 5 * rows
        self.dom_meta = -(-rows // 8) * 8

    def types(self, step):
        extra = (self.dom_meta, META) if step == 0 else (0, 0)
        far, one = self.quarter * self.n + extra[0], self.n + extra[1]
        shapes = [far] + [one] * (self.lanes - 1)
        return [pltpu.VMEM((length, self.w), jnp.float32) for length in shapes]


def items_of(plan, step, got, meta):
    color = step % COLORS
    out = []
    for p in range(plan.quarter):
        line = plan.quarter * plan.n + color * plan.quarter + p
        out.append((meta[0], line, got[0], p * plan.n))
    for lane in range(1, plan.lanes):
        out.append((meta[lane], plan.n + color, got[lane], 0))
    return out


def subtract(plan, value, row, items):
    for meta, line, got, start in items:
        here = meta[pl.ds(line, 1), :] == row
        value = value - jnp.where(here, got[pl.ds(start, plan.n), :], 0.0)
    return value


def lanes_of(plan, refs):
    return refs[: plan.lanes], refs[plan.lanes :]


def products(plan, step, table, changes, coupling, sends):
    parity = lax.rem(lax.axis_index("dom"), 2)
    far, near = sends[0], sends[plan.group :]
    terms = []
    for p in range(plan.quarter):
        at = step % COLORS * plan.quarter + p
        j = table[plan.order + at]
        both = dot(
            changes[p],
            jnp.concatenate([coupling[j, 5 - parity], coupling[j, 4 + parity]], axis=1),
        )
        far[pl.ds(p * plan.n, plan.n), :] = both[:, : plan.w]
        near[p][pl.ds(0, plan.n), :] = both[:, plan.w :]
        both = dot(changes[p], jnp.concatenate([coupling[j, 2], coupling[j, 3]], axis=1))
        for k in range(2):
            terms.append((table[plan.slot + 2 * at + k], both[:, k * plan.w : (k + 1) * plan.w]))
    for lane, s in enumerate(plan.distances):
        total = jnp.zeros((plan.n, plan.w), jnp.float32)
        for slot, term in terms:
            total = total + jnp.where(slot == s, term, 0.0)
        sends[1 + lane][pl.ds(0, plan.n), :] = total


def first_kernel(plan, *refs):
    hbm, outs, scratch = refs[:8], refs[8 : 14 + plan.lanes], refs[14 + plan.lanes :]
    table, coupling, diag, rhs, sol, change = outs[:6]
    sends = outs[6:]
    color, local_target, group_peer, group_list, dom_target = scratch[:5]
    sems = scratch[5]
    targets = (color, group_peer, group_list, dom_target, local_target, rhs, diag, coupling)
    pieces = list(zip(hbm[:5], targets[:5]))
    for src, dst in zip(hbm[5:], targets[5:]):
        pieces += [(src.at[r], dst.at[r]) for r in range(plan.rows)]
    copies = [
        pltpu.make_async_copy(src, dst, sems.at[i]) for i, (src, dst) in enumerate(pieces)
    ]
    for copy in copies:
        copy.start()
    for copy in copies[:5]:
        copy.wait()
    me = lax.axis_index("sub")
    parity = lax.rem(lax.axis_index("dom"), 2)
    colors = [color[i] for i in range(plan.rows)]
    for i in range(plan.rows):
        before = jnp.int32(0)
        for e in range(i):
            before = before + (colors[e] == colors[i]).astype(jnp.int32)
        at = colors[i] * plan.quarter + before
        table[plan.order + at] = i
        for k in range(2):
            table[plan.local + 2 * at + k] = local_target[k, i]
            table[plan.slot + 2 * at + k] = me ^ group_peer[k, i]
    for copy in copies[5 : 5 + 2 * plan.rows]:
        copy.wait()
    changes = []
    for p in range(plan.quarter):
        j = table[plan.order + p]
        new = dot(rhs[j].astype(jnp.bfloat16), diag[j])
        sol[p] = new
        changes.append(new.astype(jnp.bfloat16))
        change[p] = changes[p]
    for copy in copies[5 + 2 * plan.rows :]:
        copy.wait()
    products(plan, 0, table, changes, coupling, sends)
    line = lax.broadcasted_iota(jnp.int32, (META, plan.w), 0)
    for lane, s in enumerate(plan.distances):
        meta = jnp.full((META, plan.w), -1, jnp.int32)
        for c in range(COLORS):
            meta = jnp.where(line == c, group_list[0, c, me ^ s], meta)
        sends[1 + lane][pl.ds(plan.n, META), :] = meta.astype(jnp.float32)
    for p in range(plan.quarter):
        meta = jnp.full((META, plan.w), -1, jnp.int32)
        for c in range(COLORS):
            at = c * plan.quarter + p
            meta = jnp.where(line == c, dom_target[parity, table[plan.order + at]], meta)
        sends[plan.group + p][pl.ds(plan.n, META), :] = meta.astype(jnp.float32)
    line = lax.broadcasted_iota(jnp.int32, (plan.dom_meta, plan.w), 0)
    meta = jnp.full((plan.dom_meta, plan.w), -1, jnp.int32)
    for at in range(plan.rows):
        meta = jnp.where(line == at, dom_target[1 - parity, table[plan.order + at]], meta)
    sends[0][pl.ds(plan.quarter * plan.n, plan.dom_meta), :] = meta.astype(jnp.float32)


def step_kernel(plan, step, table, resid, diag, coupling, *refs):
    got, refs = lanes_of(plan, refs)
    meta, refs = lanes_of(plan, refs)
    has_old = step >= COLORS
    if has_old:
        old, refs = refs[0], refs[1:]
    sol, change = refs[:2]
    items = items_of(plan, step - 1, got, meta)
    changes = []
    for p in range(plan.quarter):
        j = table[plan.order + step % COLORS * plan.quarter + p]
        value = subtract(plan, resid[j], j.astype(jnp.float32), items)
        new = dot(value.astype(jnp.bfloat16), diag[j])
        sol[p] = new
        if has_old:
            new = new - old[p]
        changes.append(new.astype(jnp.bfloat16))
        change[p] = changes[p]
    products(plan, step, table, changes, coupling, refs[2:])


def local_kernel(plan, step, last, table, resid, coupling, change, *refs):
    items = []
    if step > 0:
        got, refs = lanes_of(plan, refs)
        meta, refs = lanes_of(plan, refs)
        items = items_of(plan, step - 1, got, meta)
    if last:
        sols, refs = refs[:COLORS], refs[COLORS:]
    out = refs[0]
    for r in range(plan.rows):
        out[r] = subtract(plan, resid[r], jnp.float32(r), items)
    for p in range(plan.quarter):
        at = step % COLORS * plan.quarter + p
        j = table[plan.order + at]
        both = dot(change[p], jnp.concatenate([coupling[j, 0], coupling[j, 1]], axis=1))
        for k in range(2):
            t = table[plan.local + 2 * at + k]
            out[t] = out[t] - both[:, k * plan.w : (k + 1) * plan.w]
    if last:
        for c in range(COLORS):
            for p in range(plan.quarter):
                refs[1][table[plan.order + c * plan.quarter + p]] = sols[c][p]


def final_kernel(plan, step, resid, *refs):
    got, refs = lanes_of(plan, refs)
    meta, refs = lanes_of(plan, refs)
    items = items_of(plan, step, got, meta)
    out, rows, sems = refs
    copies = []
    for r in range(plan.rows):
        rows[r] = subtract(plan, resid[r], jnp.float32(r), items)
        copies.append(pltpu.make_async_copy(rows.at[r], out.at[r], sems.at[r]))
        copies[r].start()
    for copy in copies:
        copy.wait()


def on_device(coupling, diag_inv, rhs, color, local_target, group_peer, group_list, dom_target):
    rows, rhs_count, width = rhs.shape
    doms, group = lax.axis_size("dom"), lax.axis_size("sub")
    assert group & (group - 1) == 0 and doms % 2 == 0
    plan = Plan(rows, rhs_count, width, group)
    f32 = jnp.float32
    near_pairs = [(i, i ^ 1) for i in range(doms)]
    far_pairs = [(i, (i + 1 if i % 2 else i - 1) % doms) for i in range(doms)]
    params = pltpu.CompilerParams(vmem_limit_bytes=16 * 1024 * 1024)

    def call(body, name, ins, in_specs, outs, **kw):
        smem = [getattr(o, "memory_space", None) == pltpu.SMEM for o in outs]
        out_specs = kw.pop("out_specs", [SMEM if s else VMEM for s in smem])
        return pl.pallas_call(
            body,
            name=name,
            in_specs=in_specs + [VMEM] * (len(ins) - len(in_specs)),
            out_specs=out_specs,
            out_shape=outs,
            compiler_params=params,
            **kw,
        )(*ins)

    def exchange(sends):
        got = [lax.ppermute(sends[0], "dom", far_pairs)]
        for send, s in zip(sends[1:group], plan.distances):
            got.append(lax.ppermute(send, "sub", [(i, i ^ s) for i in range(group)]))
        return got + [lax.ppermute(send, "dom", near_pairs) for send in sends[group:]]

    sol_t = pltpu.VMEM((plan.quarter, plan.n, plan.w), f32)
    change_t = pltpu.VMEM((plan.quarter, plan.n, plan.w), jnp.bfloat16)
    resid_t = pltpu.VMEM(rhs.shape, f32)
    tables = [color, group_peer.T, group_list, dom_target.T, local_target.T]
    hbm = [pltpu.with_memory_space_constraint(a, pltpu.HBM) for a in tables + [rhs, diag_inv, coupling]]
    table_scratch = [tables[i].shape for i in (0, 4, 1, 2, 3)]
    table, tiles, diags, resid, sol, change, *sends = call(
        functools.partial(first_kernel, plan),
        "first",
        hbm,
        [HBM] * len(hbm),
        [
            pltpu.SMEM((plan.table,), jnp.int32),
            pltpu.VMEM(coupling.shape, coupling.dtype),
            pltpu.VMEM(diag_inv.shape, diag_inv.dtype),
            resid_t,
            sol_t,
            change_t,
        ]
        + plan.types(0),
        scratch_shapes=[pltpu.SMEM(shape, jnp.int32) for shape in table_scratch]
        + [pltpu.SemaphoreType.DMA((5 + 3 * rows,))],
    )
    sols = [sol]
    got = meta = None
    steps = SWEEPS * COLORS
    for step in range(steps):
        c = step % COLORS
        if step > 0:
            ins = [table, resid, diags, tiles, *got, *meta]
            if step >= COLORS:
                ins.append(sols[c])
            sol, change, *sends = call(
                functools.partial(step_kernel, plan, step),
                f"step{step}",
                ins,
                [SMEM],
                [sol_t, change_t] + plan.types(step),
            )
            sols[c:] = [sol] + sols[c + 1 :]
        last = step == steps - 1
        ins = [table, resid, tiles, change]
        if step > 0:
            ins += [*got, *meta]
        if last:
            ins += sols
        resid, *rest = call(
            functools.partial(local_kernel, plan, step, last),
            f"local{step}",
            ins,
            [SMEM],
            [resid_t] + ([jax.ShapeDtypeStruct(rhs.shape, f32)] if last else []),
            input_output_aliases={1: 0},
        )
        got = exchange(sends)
        if step == 0:
            meta = got
    (defect,) = call(
        functools.partial(final_kernel, plan, steps - 1),
        "final",
        [resid, *got, *meta],
        [],
        [jax.ShapeDtypeStruct(rhs.shape, f32)],
        out_specs=[HBM],
        scratch_shapes=[pltpu.VMEM(rhs.shape, f32), pltpu.SemaphoreType.DMA((rows,))],
    )
    return rest[0], defect


def solution(mesh):
    placed = (
        P(("dom", "sub"), None, None, None),
        P(("dom", "sub"), None, None),
        P(("dom", "sub"), None, None),
        P(("dom", "sub")),
        P(("dom", "sub"), None),
        P(("dom", "sub"), None),
        P(("dom", "sub"), None, None),
        P(("dom", "sub"), None),
    )
    return jax.shard_map(
        on_device,
        mesh=mesh,
        in_specs=placed,
        out_specs=(P(("dom", "sub"), None, None), P(("dom", "sub"), None, None)),
        check_vma=False,
    )
```

```python
import functools

import jax
import jax.numpy as jnp
from jax import lax
from jax.experimental import pallas as pl
from jax.experimental.pallas import tpu as pltpu
from jax.sharding import PartitionSpec as P

COLORS = 4
SWEEPS = 2
META = 8

VMEM = pl.BlockSpec(memory_space=pltpu.VMEM)
SMEM = pl.BlockSpec(memory_space=pltpu.SMEM)
HBM = pl.BlockSpec(memory_space=pltpu.HBM)


def dot(a, b):
    return jnp.dot(a, b, preferred_element_type=jnp.float32)


class Plan:
    def __init__(self, rows, rhs_count, width, group):
        self.rows, self.n, self.w, self.group = rows, rhs_count, width, group
        self.quarter = rows // COLORS
        half = group // 2
        others = [(s, range(group)) for s in range(1, group) if s != half]
        self.swaps = [(half, range(half))] + others + [(half, range(half, group))]
        self.lanes = 1 + len(self.swaps) + self.quarter
        self.order, self.local, self.slot = 0, rows, 3 * rows
        self.table = 5 * rows
        self.dom_meta = -(-rows // 8) * 8

    def types(self, step):
        extra = (self.dom_meta, META) if step == 0 else (0, 0)
        far, one = self.quarter * self.n + extra[0], self.n + extra[1]
        shapes = [far] + [one] * (self.lanes - 1)
        count = len(self.swaps)
        spare = [0, 0, 8] + [32] * (count - 3) + [24] + [16] * self.quarter
        shapes = [length + more for length, more in zip(shapes, spare)]
        return [pltpu.VMEM((length, self.w), jnp.float32) for length in shapes]


def items_of(plan, step, got, meta):
    color = step % COLORS
    out = []
    for p in range(plan.quarter):
        line = plan.quarter * plan.n + color * plan.quarter + p
        out.append((meta[0], line, got[0], p * plan.n))
    for lane in range(1, plan.lanes):
        out.append((meta[lane], plan.n + color, got[lane], 0))
    return out


def subtract(plan, value, row, items):
    for meta, line, got, start in items:
        here = meta[pl.ds(line, 1), :] == row
        value = value - jnp.where(here, got[pl.ds(start, plan.n), :], 0.0)
    return value


def lanes_of(plan, refs):
    return refs[: plan.lanes], refs[plan.lanes :]


def products(plan, step, table, changes, coupling, sends):
    parity = lax.rem(lax.axis_index("dom"), 2)
    far, near = sends[0], sends[1 + len(plan.swaps) :]
    terms = []
    for p in range(plan.quarter):
        at = step % COLORS * plan.quarter + p
        j = table[plan.order + at]
        both = dot(
            changes[p],
            jnp.concatenate([coupling[j, 5 - parity], coupling[j, 4 + parity]], axis=1),
        )
        far[pl.ds(p * plan.n, plan.n), :] = both[:, : plan.w]
        near[p][pl.ds(0, plan.n), :] = both[:, plan.w :]
        both = dot(changes[p], jnp.concatenate([coupling[j, 2], coupling[j, 3]], axis=1))
        for k in range(2):
            terms.append((table[plan.slot + 2 * at + k], both[:, k * plan.w : (k + 1) * plan.w]))
    for lane, (s, _) in enumerate(plan.swaps):
        total = jnp.zeros((plan.n, plan.w), jnp.float32)
        for slot, term in terms:
            total = total + jnp.where(slot == s, term, 0.0)
        sends[1 + lane][pl.ds(0, plan.n), :] = total


def first_kernel(plan, *refs):
    last = 14 + plan.lanes
    hbm, outs, scratch = refs[:8], refs[8:last], refs[last:]
    table, coupling, diag, rhs, sol, change = outs[:6]
    sends = outs[6:]
    color, local_target, group_peer, group_list, dom_target = scratch[:5]
    sems = scratch[5]
    targets = (color, group_peer, group_list, dom_target, local_target, rhs, diag, coupling)
    copies = [
        pltpu.make_async_copy(src, dst, sems.at[i]) for i, (src, dst) in enumerate(zip(hbm, targets))
    ]
    for copy in copies:
        copy.start()
    for copy in copies[:5]:
        copy.wait()
    me = lax.axis_index("sub")
    parity = lax.rem(lax.axis_index("dom"), 2)
    colors = [color[i] for i in range(plan.rows)]
    for i in range(plan.rows):
        before = jnp.int32(0)
        for e in range(i):
            before = before + (colors[e] == colors[i]).astype(jnp.int32)
        at = colors[i] * plan.quarter + before
        table[plan.order + at] = i
        for k in range(2):
            table[plan.local + 2 * at + k] = local_target[k, i]
            table[plan.slot + 2 * at + k] = me ^ group_peer[k, i]
    copies[5].wait()
    copies[6].wait()
    changes = []
    for p in range(plan.quarter):
        j = table[plan.order + p]
        new = dot(rhs[j].astype(jnp.bfloat16), diag[j])
        sol[p] = new
        changes.append(new.astype(jnp.bfloat16))
        change[p] = changes[p]
    copies[7].wait()
    products(plan, 0, table, changes, coupling, sends)
    line = lax.broadcasted_iota(jnp.int32, (META, plan.w), 0)
    for lane, (s, _) in enumerate(plan.swaps):
        meta = jnp.full((META, plan.w), -1, jnp.int32)
        for c in range(COLORS):
            meta = jnp.where(line == c, group_list[0, c, me ^ s], meta)
        sends[1 + lane][pl.ds(plan.n, META), :] = meta.astype(jnp.float32)
    for p in range(plan.quarter):
        meta = jnp.full((META, plan.w), -1, jnp.int32)
        for c in range(COLORS):
            at = c * plan.quarter + p
            meta = jnp.where(line == c, dom_target[parity, table[plan.order + at]], meta)
        sends[1 + len(plan.swaps) + p][pl.ds(plan.n, META), :] = meta.astype(jnp.float32)
    line = lax.broadcasted_iota(jnp.int32, (plan.dom_meta, plan.w), 0)
    meta = jnp.full((plan.dom_meta, plan.w), -1, jnp.int32)
    for at in range(plan.rows):
        meta = jnp.where(line == at, dom_target[1 - parity, table[plan.order + at]], meta)
    sends[0][pl.ds(plan.quarter * plan.n, plan.dom_meta), :] = meta.astype(jnp.float32)


def step_kernel(plan, step, table, resid, diag, coupling, *refs):
    got, refs = lanes_of(plan, refs)
    meta, refs = lanes_of(plan, refs)
    has_old = step >= COLORS
    if has_old:
        old, refs = refs[0], refs[1:]
    sol, change = refs[:2]
    items = items_of(plan, step - 1, got, meta)
    changes = []
    for p in range(plan.quarter):
        j = table[plan.order + step % COLORS * plan.quarter + p]
        value = subtract(plan, resid[j], j.astype(jnp.float32), items)
        new = dot(value.astype(jnp.bfloat16), diag[j])
        sol[p] = new
        if has_old:
            new = new - old[p]
        changes.append(new.astype(jnp.bfloat16))
        change[p] = changes[p]
    products(plan, step, table, changes, coupling, refs[2:])


def local_kernel(plan, step, last, table, resid, coupling, change, *refs):
    items = []
    if step > 0:
        got, refs = lanes_of(plan, refs)
        meta, refs = lanes_of(plan, refs)
        items = items_of(plan, step - 1, got, meta)
    if last:
        sols, refs = refs[:COLORS], refs[COLORS:]
    out = refs[0]
    for r in range(plan.rows):
        out[r] = subtract(plan, resid[r], jnp.float32(r), items)
    for p in range(plan.quarter):
        at = step % COLORS * plan.quarter + p
        j = table[plan.order + at]
        both = dot(change[p], jnp.concatenate([coupling[j, 0], coupling[j, 1]], axis=1))
        for k in range(2):
            t = table[plan.local + 2 * at + k]
            out[t] = out[t] - both[:, k * plan.w : (k + 1) * plan.w]
    if last:
        for c in range(COLORS):
            for p in range(plan.quarter):
                refs[1][table[plan.order + c * plan.quarter + p]] = sols[c][p]


def final_kernel(plan, step, resid, *refs):
    got, refs = lanes_of(plan, refs)
    meta, refs = lanes_of(plan, refs)
    items = items_of(plan, step, got, meta)
    out, rows, sems = refs
    copies = []
    for r in range(plan.rows):
        rows[r] = subtract(plan, resid[r], jnp.float32(r), items)
        copies.append(pltpu.make_async_copy(rows.at[r], out.at[r], sems.at[r]))
        copies[r].start()
    for copy in copies:
        copy.wait()


def on_device(coupling, diag_inv, rhs, color, local_target, group_peer, group_list, dom_target):
    rows, rhs_count, width = rhs.shape
    doms, group = lax.axis_size("dom"), lax.axis_size("sub")
    assert group & (group - 1) == 0 and doms % 2 == 0
    plan = Plan(rows, rhs_count, width, group)
    f32 = jnp.float32
    near_pairs = [(i, i ^ 1) for i in range(doms)]
    far_pairs = [(i, (i + 1 if i % 2 else i - 1) % doms) for i in range(doms)]
    params = pltpu.CompilerParams(vmem_limit_bytes=16 * 1024 * 1024)

    def call(body, name, ins, in_specs, outs, **kw):
        smem = [getattr(o, "memory_space", None) == pltpu.SMEM for o in outs]
        out_specs = kw.pop("out_specs", [SMEM if s else VMEM for s in smem])
        return pl.pallas_call(
            body,
            name=name,
            in_specs=in_specs + [VMEM] * (len(ins) - len(in_specs)),
            out_specs=out_specs,
            out_shape=outs,
            compiler_params=params,
            **kw,
        )(*ins)

    def exchange(sends):
        got = [lax.ppermute(sends[0], "dom", far_pairs)]
        for send, (s, members) in zip(sends[1:], plan.swaps):
            got.append(lax.ppermute(send, "sub", [(m, m ^ s) for m in members]))
        return got + [lax.ppermute(send, "dom", near_pairs) for send in sends[len(got) :]]

    sol_t = pltpu.VMEM((plan.quarter, plan.n, plan.w), f32)
    change_t = pltpu.VMEM((plan.quarter, plan.n, plan.w), jnp.bfloat16)
    resid_t = pltpu.VMEM(rhs.shape, f32)
    tables = [color, group_peer.T, group_list, dom_target.T, local_target.T]
    hbm = [pltpu.with_memory_space_constraint(a, pltpu.HBM) for a in tables + [rhs, diag_inv, coupling]]
    table_scratch = [tables[i].shape for i in (0, 4, 1, 2, 3)]
    table, tiles, diags, resid, sol, change, *sends = call(
        functools.partial(first_kernel, plan),
        "first",
        hbm,
        [HBM] * len(hbm),
        [
            pltpu.SMEM((plan.table,), jnp.int32),
            pltpu.VMEM(coupling.shape, coupling.dtype),
            pltpu.VMEM(diag_inv.shape, diag_inv.dtype),
            resid_t,
            sol_t,
            change_t,
        ]
        + plan.types(0),
        scratch_shapes=[pltpu.SMEM(shape, jnp.int32) for shape in table_scratch]
        + [pltpu.SemaphoreType.DMA((len(hbm),))],
    )
    sols = [sol]
    got = meta = None
    steps = SWEEPS * COLORS
    for step in range(steps):
        c = step % COLORS
        if step > 0:
            ins = [table, resid, diags, tiles, *got, *meta]
            if step >= COLORS:
                ins.append(sols[c])
            sol, change, *sends = call(
                functools.partial(step_kernel, plan, step),
                f"step{step}",
                ins,
                [SMEM],
                [sol_t, change_t] + plan.types(step),
            )
            sols[c:] = [sol] + sols[c + 1 :]
        last = step == steps - 1
        ins = [table, resid, tiles, change]
        if step > 0:
            ins += [*got, *meta]
        if last:
            ins += sols
        resid, *rest = call(
            functools.partial(local_kernel, plan, step, last),
            f"local{step}",
            ins,
            [SMEM],
            [resid_t] + ([jax.ShapeDtypeStruct(rhs.shape, f32)] if last else []),
            input_output_aliases={1: 0},
        )
        got = exchange(sends)
        if step == 0:
            meta = got
    (defect,) = call(
        functools.partial(final_kernel, plan, steps - 1),
        "final",
        [resid, *got, *meta],
        [],
        [jax.ShapeDtypeStruct(rhs.shape, f32)],
        out_specs=[HBM],
        scratch_shapes=[pltpu.VMEM(rhs.shape, f32), pltpu.SemaphoreType.DMA((rows,))],
    )
    return rest[0], defect


def solution(mesh):
    placed = (
        P(("dom", "sub"), None, None, None),
        P(("dom", "sub"), None, None),
        P(("dom", "sub"), None, None),
        P(("dom", "sub")),
        P(("dom", "sub"), None),
        P(("dom", "sub"), None),
        P(("dom", "sub"), None, None),
        P(("dom", "sub"), None),
    )
    return jax.shard_map(
        on_device,
        mesh=mesh,
        in_specs=placed,
        out_specs=(P(("dom", "sub"), None, None), P(("dom", "sub"), None, None)),
        check_vma=False,
    )
```

```python
import functools

import jax
import jax.numpy as jnp
from jax import lax
from jax.experimental import pallas as pl
from jax.experimental.pallas import tpu as pltpu
from jax.sharding import PartitionSpec as P

COLORS = 4
SWEEPS = 2
META = 8

VMEM = pl.BlockSpec(memory_space=pltpu.VMEM)
SMEM = pl.BlockSpec(memory_space=pltpu.SMEM)
HBM = pl.BlockSpec(memory_space=pltpu.HBM)


def dot(a, b):
    return jnp.dot(a, b, preferred_element_type=jnp.float32)


class Plan:
    def __init__(self, rows, rhs_count, width, group):
        self.rows, self.n, self.w, self.group = rows, rhs_count, width, group
        self.quarter = rows // COLORS
        self.lanes = group + self.quarter
        self.distances = list(reversed(range(1, group)))
        self.order, self.local, self.slot = 0, rows, 3 * rows
        self.table = 5 * rows
        self.dom_meta = -(-rows // 8) * 8

    def types(self, step):
        extra = (self.dom_meta, META) if step == 0 else (0, 0)
        far, one = self.quarter * self.n + extra[0], self.n + extra[1]
        shapes = [far] + [one] * (self.lanes - 1)
        return [pltpu.VMEM((length, self.w), jnp.float32) for length in shapes]


def items_of(plan, step, got, meta):
    color = step % COLORS
    out = []
    for p in range(plan.quarter):
        line = plan.quarter * plan.n + color * plan.quarter + p
        out.append((meta[0], line, got[0], p * plan.n))
    for lane in range(1, plan.lanes):
        out.append((meta[lane], plan.n + color, got[lane], 0))
    return out


def subtract(plan, value, row, items):
    for meta, line, got, start in items:
        here = meta[pl.ds(line, 1), :] == row
        value = value - jnp.where(here, got[pl.ds(start, plan.n), :], 0.0)
    return value


def lanes_of(plan, refs):
    return refs[: plan.lanes], refs[plan.lanes :]


def products(plan, step, table, changes, coupling, sends):
    parity = lax.rem(lax.axis_index("dom"), 2)
    far, near = sends[0], sends[plan.group :]
    terms = []
    for p in range(plan.quarter):
        at = step % COLORS * plan.quarter + p
        j = table[plan.order + at]
        both = dot(
            changes[p],
            jnp.concatenate([coupling[j, 5 - parity], coupling[j, 4 + parity]], axis=1),
        )
        far[pl.ds(p * plan.n, plan.n), :] = both[:, : plan.w]
        near[p][pl.ds(0, plan.n), :] = both[:, plan.w :]
        both = dot(changes[p], jnp.concatenate([coupling[j, 2], coupling[j, 3]], axis=1))
        for k in range(2):
            terms.append((table[plan.slot + 2 * at + k], both[:, k * plan.w : (k + 1) * plan.w]))
    for lane, s in enumerate(plan.distances):
        total = jnp.zeros((plan.n, plan.w), jnp.float32)
        for slot, term in terms:
            total = total + jnp.where(slot == s, term, 0.0)
        sends[1 + lane][pl.ds(0, plan.n), :] = total


def first_kernel(plan, *refs):
    hbm, outs, scratch = refs[:8], refs[8 : 14 + plan.lanes], refs[14 + plan.lanes :]
    table, coupling, diag, rhs, sol, change = outs[:6]
    sends = outs[6:]
    color, local_target, group_peer, group_list, dom_target = scratch[:5]
    sems = scratch[5]
    targets = (color, group_peer, group_list, dom_target, local_target, rhs, diag, coupling)
    copies = [
        pltpu.make_async_copy(src, dst, sems.at[i]) for i, (src, dst) in enumerate(zip(hbm, targets))
    ]
    for copy in copies[7:] + copies[:7]:
        copy.start()
    for copy in copies[:5]:
        copy.wait()
    me = lax.axis_index("sub")
    parity = lax.rem(lax.axis_index("dom"), 2)
    colors = [color[i] for i in range(plan.rows)]
    for i in range(plan.rows):
        before = jnp.int32(0)
        for e in range(i):
            before = before + (colors[e] == colors[i]).astype(jnp.int32)
        at = colors[i] * plan.quarter + before
        table[plan.order + at] = i
        for k in range(2):
            table[plan.local + 2 * at + k] = local_target[k, i]
            table[plan.slot + 2 * at + k] = me ^ group_peer[k, i]
    copies[5].wait()
    copies[6].wait()
    changes = []
    for p in range(plan.quarter):
        j = table[plan.order + p]
        new = dot(rhs[j].astype(jnp.bfloat16), diag[j])
        sol[p] = new
        changes.append(new.astype(jnp.bfloat16))
        change[p] = changes[p]
    copies[7].wait()
    products(plan, 0, table, changes, coupling, sends)
    line = lax.broadcasted_iota(jnp.int32, (META, plan.w), 0)
    for lane, s in enumerate(plan.distances):
        meta = jnp.full((META, plan.w), -1, jnp.int32)
        for c in range(COLORS):
            meta = jnp.where(line == c, group_list[0, c, me ^ s], meta)
        sends[1 + lane][pl.ds(plan.n, META), :] = meta.astype(jnp.float32)
    for p in range(plan.quarter):
        meta = jnp.full((META, plan.w), -1, jnp.int32)
        for c in range(COLORS):
            at = c * plan.quarter + p
            meta = jnp.where(line == c, dom_target[parity, table[plan.order + at]], meta)
        sends[plan.group + p][pl.ds(plan.n, META), :] = meta.astype(jnp.float32)
    line = lax.broadcasted_iota(jnp.int32, (plan.dom_meta, plan.w), 0)
    meta = jnp.full((plan.dom_meta, plan.w), -1, jnp.int32)
    for at in range(plan.rows):
        meta = jnp.where(line == at, dom_target[1 - parity, table[plan.order + at]], meta)
    sends[0][pl.ds(plan.quarter * plan.n, plan.dom_meta), :] = meta.astype(jnp.float32)


def step_kernel(plan, step, table, resid, diag, coupling, *refs):
    got, refs = lanes_of(plan, refs)
    meta, refs = lanes_of(plan, refs)
    has_old = step >= COLORS
    if has_old:
        old, refs = refs[0], refs[1:]
    sol, change = refs[:2]
    items = items_of(plan, step - 1, got, meta)
    changes = []
    for p in range(plan.quarter):
        j = table[plan.order + step % COLORS * plan.quarter + p]
        value = subtract(plan, resid[j], j.astype(jnp.float32), items)
        new = dot(value.astype(jnp.bfloat16), diag[j])
        sol[p] = new
        if has_old:
            new = new - old[p]
        changes.append(new.astype(jnp.bfloat16))
        change[p] = changes[p]
    products(plan, step, table, changes, coupling, refs[2:])


def local_kernel(plan, step, last, table, resid, coupling, change, *refs):
    items = []
    if step > 0:
        got, refs = lanes_of(plan, refs)
        meta, refs = lanes_of(plan, refs)
        items = items_of(plan, step - 1, got, meta)
    if last:
        sols, refs = refs[:COLORS], refs[COLORS:]
    out = refs[0]
    for r in range(plan.rows):
        out[r] = subtract(plan, resid[r], jnp.float32(r), items)
    for p in range(plan.quarter):
        at = step % COLORS * plan.quarter + p
        j = table[plan.order + at]
        both = dot(change[p], jnp.concatenate([coupling[j, 0], coupling[j, 1]], axis=1))
        for k in range(2):
            t = table[plan.local + 2 * at + k]
            out[t] = out[t] - both[:, k * plan.w : (k + 1) * plan.w]
    if last:
        for c in range(COLORS):
            for p in range(plan.quarter):
                refs[1][table[plan.order + c * plan.quarter + p]] = sols[c][p]


def final_kernel(plan, step, resid, *refs):
    got, refs = lanes_of(plan, refs)
    meta, refs = lanes_of(plan, refs)
    items = items_of(plan, step, got, meta)
    out, rows, sems = refs
    copies = []
    for r in range(plan.rows):
        rows[r] = subtract(plan, resid[r], jnp.float32(r), items)
        copies.append(pltpu.make_async_copy(rows.at[r], out.at[r], sems.at[r]))
        copies[r].start()
    for copy in copies:
        copy.wait()


def on_device(coupling, diag_inv, rhs, color, local_target, group_peer, group_list, dom_target):
    rows, rhs_count, width = rhs.shape
    doms, group = lax.axis_size("dom"), lax.axis_size("sub")
    assert group & (group - 1) == 0 and doms % 2 == 0
    plan = Plan(rows, rhs_count, width, group)
    f32 = jnp.float32
    near_pairs = [(i, i ^ 1) for i in range(doms)]
    far_pairs = [(i, (i + 1 if i % 2 else i - 1) % doms) for i in range(doms)]
    params = pltpu.CompilerParams(vmem_limit_bytes=16 * 1024 * 1024)

    def call(body, name, ins, in_specs, outs, **kw):
        smem = [getattr(o, "memory_space", None) == pltpu.SMEM for o in outs]
        out_specs = kw.pop("out_specs", [SMEM if s else VMEM for s in smem])
        return pl.pallas_call(
            body,
            name=name,
            in_specs=in_specs + [VMEM] * (len(ins) - len(in_specs)),
            out_specs=out_specs,
            out_shape=outs,
            compiler_params=params,
            **kw,
        )(*ins)

    def exchange(sends):
        got = [lax.ppermute(sends[0], "dom", far_pairs)]
        for send, s in zip(sends[1:group], plan.distances):
            got.append(lax.ppermute(send, "sub", [(i, i ^ s) for i in range(group)]))
        return got + [lax.ppermute(send, "dom", near_pairs) for send in sends[group:]]

    sol_t = pltpu.VMEM((plan.quarter, plan.n, plan.w), f32)
    change_t = pltpu.VMEM((plan.quarter, plan.n, plan.w), jnp.bfloat16)
    resid_t = pltpu.VMEM(rhs.shape, f32)
    tables = [color, group_peer.T, group_list, dom_target.T, local_target.T]
    hbm = [pltpu.with_memory_space_constraint(a, pltpu.HBM) for a in tables + [rhs, diag_inv, coupling]]
    table_scratch = [tables[i].shape for i in (0, 4, 1, 2, 3)]
    table, tiles, diags, resid, sol, change, *sends = call(
        functools.partial(first_kernel, plan),
        "first",
        hbm,
        [HBM] * len(hbm),
        [
            pltpu.SMEM((plan.table,), jnp.int32),
            pltpu.VMEM(coupling.shape, coupling.dtype),
            pltpu.VMEM(diag_inv.shape, diag_inv.dtype),
            resid_t,
            sol_t,
            change_t,
        ]
        + plan.types(0),
        scratch_shapes=[pltpu.SMEM(shape, jnp.int32) for shape in table_scratch]
        + [pltpu.SemaphoreType.DMA((len(hbm),))],
    )
    sols = [sol]
    got = meta = None
    steps = SWEEPS * COLORS
    for step in range(steps):
        c = step % COLORS
        if step > 0:
            ins = [table, resid, diags, tiles, *got, *meta]
            if step >= COLORS:
                ins.append(sols[c])
            sol, change, *sends = call(
                functools.partial(step_kernel, plan, step),
                f"step{step}",
                ins,
                [SMEM],
                [sol_t, change_t] + plan.types(step),
            )
            sols[c:] = [sol] + sols[c + 1 :]
        last = step == steps - 1
        ins = [table, resid, tiles, change]
        if step > 0:
            ins += [*got, *meta]
        if last:
            ins += sols
        resid, *rest = call(
            functools.partial(local_kernel, plan, step, last),
            f"local{step}",
            ins,
            [SMEM],
            [resid_t] + ([jax.ShapeDtypeStruct(rhs.shape, f32)] if last else []),
            input_output_aliases={1: 0},
        )
        got = exchange(sends)
        if step == 0:
            meta = got
    (defect,) = call(
        functools.partial(final_kernel, plan, steps - 1),
        "final",
        [resid, *got, *meta],
        [],
        [jax.ShapeDtypeStruct(rhs.shape, f32)],
        out_specs=[HBM],
        scratch_shapes=[pltpu.VMEM(rhs.shape, f32), pltpu.SemaphoreType.DMA((rows,))],
    )
    return rest[0], defect


def solution(mesh):
    placed = (
        P(("dom", "sub"), None, None, None),
        P(("dom", "sub"), None, None),
        P(("dom", "sub"), None, None),
        P(("dom", "sub")),
        P(("dom", "sub"), None),
        P(("dom", "sub"), None),
        P(("dom", "sub"), None, None),
        P(("dom", "sub"), None),
    )
    return jax.shard_map(
        on_device,
        mesh=mesh,
        in_specs=placed,
        out_specs=(P(("dom", "sub"), None, None), P(("dom", "sub"), None, None)),
        check_vma=False,
    )
```

```python
import functools

import jax
import jax.numpy as jnp
from jax import lax
from jax.experimental import pallas as pl
from jax.experimental.pallas import tpu as pltpu
from jax.sharding import PartitionSpec as P

COLORS = 4
SWEEPS = 2
META = 8

VMEM = pl.BlockSpec(memory_space=pltpu.VMEM)
SMEM = pl.BlockSpec(memory_space=pltpu.SMEM)
HBM = pl.BlockSpec(memory_space=pltpu.HBM)


def dot(a, b):
    return jnp.dot(a, b, preferred_element_type=jnp.float32)


class Plan:
    def __init__(self, rows, rhs_count, width, group):
        self.rows, self.n, self.w, self.group = rows, rhs_count, width, group
        self.quarter = rows // COLORS
        self.lanes = group + self.quarter
        self.distances = list(reversed(range(1, group)))
        self.order, self.local, self.slot = 0, rows, 3 * rows
        self.table = 5 * rows
        self.dom_meta = -(-rows // 8) * 8

    def types(self, step):
        extra = (self.dom_meta, META) if step == 0 else (0, 0)
        far, one = self.quarter * self.n + extra[0], self.n + extra[1]
        shapes = [far] + [one] * (self.lanes - 1)
        return [pltpu.VMEM((length, self.w), jnp.float32) for length in shapes]


def items_of(plan, step, got, meta):
    color = step % COLORS
    out = []
    for p in range(plan.quarter):
        line = plan.quarter * plan.n + color * plan.quarter + p
        out.append((meta[0], line, got[0], p * plan.n))
    for lane in range(1, plan.lanes):
        out.append((meta[lane], plan.n + color, got[lane], 0))
    return out


def subtract(plan, value, row, items):
    for meta, line, got, start in items:
        here = meta[pl.ds(line, 1), :] == row
        value = value - jnp.where(here, got[pl.ds(start, plan.n), :], 0.0)
    return value


def lanes_of(plan, refs):
    return refs[: plan.lanes], refs[plan.lanes :]


def products(plan, step, table, changes, coupling, sends):
    parity = lax.rem(lax.axis_index("dom"), 2)
    far, near = sends[0], sends[plan.group :]
    terms = []
    for p in range(plan.quarter):
        at = step % COLORS * plan.quarter + p
        j = table[plan.order + at]
        tiles = [coupling[j, k] for k in (2, 3, 5 - parity, 4 + parity)]
        wide = dot(changes[p], jnp.concatenate(tiles, axis=1))
        parts = [wide[:, k * plan.w : (k + 1) * plan.w] for k in range(4)]
        far[pl.ds(p * plan.n, plan.n), :] = parts[2]
        near[p][pl.ds(0, plan.n), :] = parts[3]
        for k in range(2):
            terms.append((table[plan.slot + 2 * at + k], parts[k]))
    for lane, s in enumerate(plan.distances):
        total = jnp.zeros((plan.n, plan.w), jnp.float32)
        for slot, term in terms:
            total = total + jnp.where(slot == s, term, 0.0)
        sends[1 + lane][pl.ds(0, plan.n), :] = total


def first_kernel(plan, *refs):
    hbm, outs, scratch = refs[:8], refs[8 : 14 + plan.lanes], refs[14 + plan.lanes :]
    table, coupling, diag, rhs, sol, change = outs[:6]
    sends = outs[6:]
    color, local_target, group_peer, group_list, dom_target = scratch[:5]
    sems = scratch[5]
    targets = (color, group_peer, group_list, dom_target, local_target, rhs, diag, coupling)
    copies = [
        pltpu.make_async_copy(src, dst, sems.at[i]) for i, (src, dst) in enumerate(zip(hbm, targets))
    ]
    for copy in copies[7:] + copies[:7]:
        copy.start()
    for copy in copies[:5]:
        copy.wait()
    me = lax.axis_index("sub")
    parity = lax.rem(lax.axis_index("dom"), 2)
    colors = [color[i] for i in range(plan.rows)]
    for i in range(plan.rows):
        before = jnp.int32(0)
        for e in range(i):
            before = before + (colors[e] == colors[i]).astype(jnp.int32)
        at = colors[i] * plan.quarter + before
        table[plan.order + at] = i
        for k in range(2):
            table[plan.local + 2 * at + k] = local_target[k, i]
            table[plan.slot + 2 * at + k] = me ^ group_peer[k, i]
    copies[5].wait()
    copies[6].wait()
    changes = []
    for p in range(plan.quarter):
        j = table[plan.order + p]
        new = dot(rhs[j].astype(jnp.bfloat16), diag[j])
        sol[p] = new
        changes.append(new.astype(jnp.bfloat16))
        change[p] = changes[p]
    copies[7].wait()
    products(plan, 0, table, changes, coupling, sends)
    line = lax.broadcasted_iota(jnp.int32, (META, plan.w), 0)
    for lane, s in enumerate(plan.distances):
        meta = jnp.full((META, plan.w), -1, jnp.int32)
        for c in range(COLORS):
            meta = jnp.where(line == c, group_list[0, c, me ^ s], meta)
        sends[1 + lane][pl.ds(plan.n, META), :] = meta.astype(jnp.float32)
    for p in range(plan.quarter):
        meta = jnp.full((META, plan.w), -1, jnp.int32)
        for c in range(COLORS):
            at = c * plan.quarter + p
            meta = jnp.where(line == c, dom_target[parity, table[plan.order + at]], meta)
        sends[plan.group + p][pl.ds(plan.n, META), :] = meta.astype(jnp.float32)
    line = lax.broadcasted_iota(jnp.int32, (plan.dom_meta, plan.w), 0)
    meta = jnp.full((plan.dom_meta, plan.w), -1, jnp.int32)
    for at in range(plan.rows):
        meta = jnp.where(line == at, dom_target[1 - parity, table[plan.order + at]], meta)
    sends[0][pl.ds(plan.quarter * plan.n, plan.dom_meta), :] = meta.astype(jnp.float32)


def step_kernel(plan, step, table, resid, diag, coupling, *refs):
    got, refs = lanes_of(plan, refs)
    meta, refs = lanes_of(plan, refs)
    has_old = step >= COLORS
    if has_old:
        old, refs = refs[0], refs[1:]
    sol, change = refs[:2]
    items = items_of(plan, step - 1, got, meta)
    changes = []
    for p in range(plan.quarter):
        j = table[plan.order + step % COLORS * plan.quarter + p]
        value = subtract(plan, resid[j], j.astype(jnp.float32), items)
        new = dot(value.astype(jnp.bfloat16), diag[j])
        sol[p] = new
        if has_old:
            new = new - old[p]
        changes.append(new.astype(jnp.bfloat16))
        change[p] = changes[p]
    products(plan, step, table, changes, coupling, refs[2:])


def local_kernel(plan, step, last, table, resid, coupling, change, *refs):
    items = []
    if step > 0:
        got, refs = lanes_of(plan, refs)
        meta, refs = lanes_of(plan, refs)
        items = items_of(plan, step - 1, got, meta)
    if last:
        sols, refs = refs[:COLORS], refs[COLORS:]
    out = refs[0]
    for r in range(plan.rows):
        out[r] = subtract(plan, resid[r], jnp.float32(r), items)
    for p in range(plan.quarter):
        at = step % COLORS * plan.quarter + p
        j = table[plan.order + at]
        both = dot(change[p], jnp.concatenate([coupling[j, 0], coupling[j, 1]], axis=1))
        for k in range(2):
            t = table[plan.local + 2 * at + k]
            out[t] = out[t] - both[:, k * plan.w : (k + 1) * plan.w]
    if last:
        for c in range(COLORS):
            for p in range(plan.quarter):
                refs[1][table[plan.order + c * plan.quarter + p]] = sols[c][p]


def final_kernel(plan, step, resid, *refs):
    got, refs = lanes_of(plan, refs)
    meta, refs = lanes_of(plan, refs)
    items = items_of(plan, step, got, meta)
    out, rows, sems = refs
    copies = []
    for r in range(plan.rows):
        rows[r] = subtract(plan, resid[r], jnp.float32(r), items)
        copies.append(pltpu.make_async_copy(rows.at[r], out.at[r], sems.at[r]))
        copies[r].start()
    for copy in copies:
        copy.wait()


def on_device(coupling, diag_inv, rhs, color, local_target, group_peer, group_list, dom_target):
    rows, rhs_count, width = rhs.shape
    doms, group = lax.axis_size("dom"), lax.axis_size("sub")
    assert group & (group - 1) == 0 and doms % 2 == 0
    plan = Plan(rows, rhs_count, width, group)
    f32 = jnp.float32
    near_pairs = [(i, i ^ 1) for i in range(doms)]
    far_pairs = [(i, (i + 1 if i % 2 else i - 1) % doms) for i in range(doms)]
    params = pltpu.CompilerParams(vmem_limit_bytes=16 * 1024 * 1024)

    def call(body, name, ins, in_specs, outs, **kw):
        smem = [getattr(o, "memory_space", None) == pltpu.SMEM for o in outs]
        out_specs = kw.pop("out_specs", [SMEM if s else VMEM for s in smem])
        return pl.pallas_call(
            body,
            name=name,
            in_specs=in_specs + [VMEM] * (len(ins) - len(in_specs)),
            out_specs=out_specs,
            out_shape=outs,
            compiler_params=params,
            **kw,
        )(*ins)

    def exchange(sends):
        got = [lax.ppermute(sends[0], "dom", far_pairs)]
        for send, s in zip(sends[1:group], plan.distances):
            got.append(lax.ppermute(send, "sub", [(i, i ^ s) for i in range(group)]))
        return got + [lax.ppermute(send, "dom", near_pairs) for send in sends[group:]]

    sol_t = pltpu.VMEM((plan.quarter, plan.n, plan.w), f32)
    change_t = pltpu.VMEM((plan.quarter, plan.n, plan.w), jnp.bfloat16)
    resid_t = pltpu.VMEM(rhs.shape, f32)
    tables = [color, group_peer.T, group_list, dom_target.T, local_target.T]
    hbm = [pltpu.with_memory_space_constraint(a, pltpu.HBM) for a in tables + [rhs, diag_inv, coupling]]
    table_scratch = [tables[i].shape for i in (0, 4, 1, 2, 3)]
    table, tiles, diags, resid, sol, change, *sends = call(
        functools.partial(first_kernel, plan),
        "first",
        hbm,
        [HBM] * len(hbm),
        [
            pltpu.SMEM((plan.table,), jnp.int32),
            pltpu.VMEM(coupling.shape, coupling.dtype),
            pltpu.VMEM(diag_inv.shape, diag_inv.dtype),
            resid_t,
            sol_t,
            change_t,
        ]
        + plan.types(0),
        scratch_shapes=[pltpu.SMEM(shape, jnp.int32) for shape in table_scratch]
        + [pltpu.SemaphoreType.DMA((len(hbm),))],
    )
    sols = [sol]
    got = meta = None
    steps = SWEEPS * COLORS
    for step in range(steps):
        c = step % COLORS
        if step > 0:
            ins = [table, resid, diags, tiles, *got, *meta]
            if step >= COLORS:
                ins.append(sols[c])
            sol, change, *sends = call(
                functools.partial(step_kernel, plan, step),
                f"step{step}",
                ins,
                [SMEM],
                [sol_t, change_t] + plan.types(step),
            )
            sols[c:] = [sol] + sols[c + 1 :]
        last = step == steps - 1
        ins = [table, resid, tiles, change]
        if step > 0:
            ins += [*got, *meta]
        if last:
            ins += sols
        resid, *rest = call(
            functools.partial(local_kernel, plan, step, last),
            f"local{step}",
            ins,
            [SMEM],
            [resid_t] + ([jax.ShapeDtypeStruct(rhs.shape, f32)] if last else []),
            input_output_aliases={1: 0},
        )
        got = exchange(sends)
        if step == 0:
            meta = got
    (defect,) = call(
        functools.partial(final_kernel, plan, steps - 1),
        "final",
        [resid, *got, *meta],
        [],
        [jax.ShapeDtypeStruct(rhs.shape, f32)],
        out_specs=[HBM],
        scratch_shapes=[pltpu.VMEM(rhs.shape, f32), pltpu.SemaphoreType.DMA((rows,))],
    )
    return rest[0], defect


def solution(mesh):
    placed = (
        P(("dom", "sub"), None, None, None),
        P(("dom", "sub"), None, None),
        P(("dom", "sub"), None, None),
        P(("dom", "sub")),
        P(("dom", "sub"), None),
        P(("dom", "sub"), None),
        P(("dom", "sub"), None, None),
        P(("dom", "sub"), None),
    )
    return jax.shard_map(
        on_device,
        mesh=mesh,
        in_specs=placed,
        out_specs=(P(("dom", "sub"), None, None), P(("dom", "sub"), None, None)),
        check_vma=False,
    )
```

```python
import functools

import jax
import jax.numpy as jnp
from jax import lax
from jax.experimental import pallas as pl
from jax.experimental.pallas import tpu as pltpu
from jax.sharding import PartitionSpec as P

COLORS = 4
SWEEPS = 2
META = 8

VMEM = pl.BlockSpec(memory_space=pltpu.VMEM)
SMEM = pl.BlockSpec(memory_space=pltpu.SMEM)
HBM = pl.BlockSpec(memory_space=pltpu.HBM)


def dot(a, b):
    return jnp.dot(a, b, preferred_element_type=jnp.float32)


class Plan:
    def __init__(self, rows, rhs_count, width, group):
        self.rows, self.n, self.w, self.group = rows, rhs_count, width, group
        self.quarter = rows // COLORS
        self.lanes = group + self.quarter
        self.distances = list(reversed(range(1, group)))
        self.order, self.local, self.slot = 0, rows, 3 * rows
        self.table = 5 * rows
        self.dom_meta = -(-rows // 8) * 8

    def types(self, step):
        extra = (self.dom_meta, META) if step == 0 else (0, 0)
        far, one = self.quarter * self.n + extra[0], self.n + extra[1]
        shapes = [far] + [one] * (self.lanes - 1)
        return [pltpu.VMEM((length, self.w), jnp.float32) for length in shapes]


def items_of(plan, step, got, meta):
    color = step % COLORS
    out = []
    for p in range(plan.quarter):
        line = plan.quarter * plan.n + color * plan.quarter + p
        out.append((meta[0], line, got[0], p * plan.n))
    for lane in range(1, plan.lanes):
        out.append((meta[lane], plan.n + color, got[lane], 0))
    return out


def subtract(plan, value, row, items):
    for meta, line, got, start in items:
        here = meta[pl.ds(line, 1), :] == row
        value = value - jnp.where(here, got[pl.ds(start, plan.n), :], 0.0)
    return value


def lanes_of(plan, refs):
    return refs[: plan.lanes], refs[plan.lanes :]


def products(plan, step, table, changes, coupling, sends):
    parity = lax.rem(lax.axis_index("dom"), 2)
    far, near = sends[0], sends[plan.group :]
    terms = []
    for p in range(plan.quarter):
        at = step % COLORS * plan.quarter + p
        j = table[plan.order + at]
        both = dot(
            changes[p],
            jnp.concatenate([coupling[j, 5 - parity], coupling[j, 4 + parity]], axis=1),
        )
        far[pl.ds(p * plan.n, plan.n), :] = both[:, : plan.w]
        near[p][pl.ds(0, plan.n), :] = both[:, plan.w :]
        both = dot(changes[p], jnp.concatenate([coupling[j, 2], coupling[j, 3]], axis=1))
        for k in range(2):
            terms.append((table[plan.slot + 2 * at + k], both[:, k * plan.w : (k + 1) * plan.w]))
    for lane, s in enumerate(plan.distances):
        total = jnp.zeros((plan.n, plan.w), jnp.float32)
        for slot, term in terms:
            total = total + jnp.where(slot == s, term, 0.0)
        sends[1 + lane][pl.ds(0, plan.n), :] = total


def first_kernel(plan, *refs):
    hbm, outs, scratch = refs[:8], refs[8 : 14 + plan.lanes], refs[14 + plan.lanes :]
    table, coupling, diag, rhs, sol, change = outs[:6]
    sends = outs[6:]
    color, local_target, group_peer, group_list, dom_target = scratch[:5]
    sems = scratch[5]
    targets = (color, group_peer, group_list, dom_target, local_target, rhs, diag, coupling)
    pieces = list(zip(hbm[:7], targets[:7]))
    for part in (pl.ds(2, coupling.shape[1] - 2), pl.ds(0, 2)):
        pieces.append((hbm[7].at[:, part], coupling.at[:, part]))
    copies = [pltpu.make_async_copy(src, dst, sems.at[i]) for i, (src, dst) in enumerate(pieces)]
    for copy in copies[7:8] + copies[:7] + copies[8:]:
        copy.start()
    for copy in copies[:5]:
        copy.wait()
    me = lax.axis_index("sub")
    parity = lax.rem(lax.axis_index("dom"), 2)
    colors = [color[i] for i in range(plan.rows)]
    for i in range(plan.rows):
        before = jnp.int32(0)
        for e in range(i):
            before = before + (colors[e] == colors[i]).astype(jnp.int32)
        at = colors[i] * plan.quarter + before
        table[plan.order + at] = i
        for k in range(2):
            table[plan.local + 2 * at + k] = local_target[k, i]
            table[plan.slot + 2 * at + k] = me ^ group_peer[k, i]
    copies[5].wait()
    copies[6].wait()
    changes = []
    for p in range(plan.quarter):
        j = table[plan.order + p]
        new = dot(rhs[j].astype(jnp.bfloat16), diag[j])
        sol[p] = new
        changes.append(new.astype(jnp.bfloat16))
        change[p] = changes[p]
    copies[7].wait()
    products(plan, 0, table, changes, coupling, sends)
    line = lax.broadcasted_iota(jnp.int32, (META, plan.w), 0)
    for lane, s in enumerate(plan.distances):
        meta = jnp.full((META, plan.w), -1, jnp.int32)
        for c in range(COLORS):
            meta = jnp.where(line == c, group_list[0, c, me ^ s], meta)
        sends[1 + lane][pl.ds(plan.n, META), :] = meta.astype(jnp.float32)
    for p in range(plan.quarter):
        meta = jnp.full((META, plan.w), -1, jnp.int32)
        for c in range(COLORS):
            at = c * plan.quarter + p
            meta = jnp.where(line == c, dom_target[parity, table[plan.order + at]], meta)
        sends[plan.group + p][pl.ds(plan.n, META), :] = meta.astype(jnp.float32)
    line = lax.broadcasted_iota(jnp.int32, (plan.dom_meta, plan.w), 0)
    meta = jnp.full((plan.dom_meta, plan.w), -1, jnp.int32)
    for at in range(plan.rows):
        meta = jnp.where(line == at, dom_target[1 - parity, table[plan.order + at]], meta)
    sends[0][pl.ds(plan.quarter * plan.n, plan.dom_meta), :] = meta.astype(jnp.float32)
    copies[8].wait()


def step_kernel(plan, step, table, resid, diag, coupling, *refs):
    got, refs = lanes_of(plan, refs)
    meta, refs = lanes_of(plan, refs)
    has_old = step >= COLORS
    if has_old:
        old, refs = refs[0], refs[1:]
    sol, change = refs[:2]
    items = items_of(plan, step - 1, got, meta)
    changes = []
    for p in range(plan.quarter):
        j = table[plan.order + step % COLORS * plan.quarter + p]
        value = subtract(plan, resid[j], j.astype(jnp.float32), items)
        new = dot(value.astype(jnp.bfloat16), diag[j])
        sol[p] = new
        if has_old:
            new = new - old[p]
        changes.append(new.astype(jnp.bfloat16))
        change[p] = changes[p]
    products(plan, step, table, changes, coupling, refs[2:])


def local_kernel(plan, step, last, table, resid, coupling, change, *refs):
    items = []
    if step > 0:
        got, refs = lanes_of(plan, refs)
        meta, refs = lanes_of(plan, refs)
        items = items_of(plan, step - 1, got, meta)
    if last:
        sols, refs = refs[:COLORS], refs[COLORS:]
    out = refs[0]
    for r in range(plan.rows):
        out[r] = subtract(plan, resid[r], jnp.float32(r), items)
    for p in range(plan.quarter):
        at = step % COLORS * plan.quarter + p
        j = table[plan.order + at]
        both = dot(change[p], jnp.concatenate([coupling[j, 0], coupling[j, 1]], axis=1))
        for k in range(2):
            t = table[plan.local + 2 * at + k]
            out[t] = out[t] - both[:, k * plan.w : (k + 1) * plan.w]
    if last:
        for c in range(COLORS):
            for p in range(plan.quarter):
                refs[1][table[plan.order + c * plan.quarter + p]] = sols[c][p]


def final_kernel(plan, step, resid, *refs):
    got, refs = lanes_of(plan, refs)
    meta, refs = lanes_of(plan, refs)
    items = items_of(plan, step, got, meta)
    out, rows, sems = refs
    copies = []
    for r in range(plan.rows):
        rows[r] = subtract(plan, resid[r], jnp.float32(r), items)
        copies.append(pltpu.make_async_copy(rows.at[r], out.at[r], sems.at[r]))
        copies[r].start()
    for copy in copies:
        copy.wait()


def on_device(coupling, diag_inv, rhs, color, local_target, group_peer, group_list, dom_target):
    rows, rhs_count, width = rhs.shape
    doms, group = lax.axis_size("dom"), lax.axis_size("sub")
    assert group & (group - 1) == 0 and doms % 2 == 0
    plan = Plan(rows, rhs_count, width, group)
    f32 = jnp.float32
    near_pairs = [(i, i ^ 1) for i in range(doms)]
    far_pairs = [(i, (i + 1 if i % 2 else i - 1) % doms) for i in range(doms)]
    params = pltpu.CompilerParams(vmem_limit_bytes=16 * 1024 * 1024)

    def call(body, name, ins, in_specs, outs, **kw):
        smem = [getattr(o, "memory_space", None) == pltpu.SMEM for o in outs]
        out_specs = kw.pop("out_specs", [SMEM if s else VMEM for s in smem])
        return pl.pallas_call(
            body,
            name=name,
            in_specs=in_specs + [VMEM] * (len(ins) - len(in_specs)),
            out_specs=out_specs,
            out_shape=outs,
            compiler_params=params,
            **kw,
        )(*ins)

    def exchange(sends):
        got = [lax.ppermute(sends[0], "dom", far_pairs)]
        for send, s in zip(sends[1:group], plan.distances):
            got.append(lax.ppermute(send, "sub", [(i, i ^ s) for i in range(group)]))
        return got + [lax.ppermute(send, "dom", near_pairs) for send in sends[group:]]

    sol_t = pltpu.VMEM((plan.quarter, plan.n, plan.w), f32)
    change_t = pltpu.VMEM((plan.quarter, plan.n, plan.w), jnp.bfloat16)
    resid_t = pltpu.VMEM(rhs.shape, f32)
    tables = [color, group_peer.T, group_list, dom_target.T, local_target.T]
    hbm = [pltpu.with_memory_space_constraint(a, pltpu.HBM) for a in tables + [rhs, diag_inv, coupling]]
    table_scratch = [tables[i].shape for i in (0, 4, 1, 2, 3)]
    table, tiles, diags, resid, sol, change, *sends = call(
        functools.partial(first_kernel, plan),
        "first",
        hbm,
        [HBM] * len(hbm),
        [
            pltpu.SMEM((plan.table,), jnp.int32),
            pltpu.VMEM(coupling.shape, coupling.dtype),
            pltpu.VMEM(diag_inv.shape, diag_inv.dtype),
            resid_t,
            sol_t,
            change_t,
        ]
        + plan.types(0),
        scratch_shapes=[pltpu.SMEM(shape, jnp.int32) for shape in table_scratch]
        + [pltpu.SemaphoreType.DMA((len(hbm) + 1,))],
    )
    sols = [sol]
    got = meta = None
    steps = SWEEPS * COLORS
    for step in range(steps):
        c = step % COLORS
        if step > 0:
            ins = [table, resid, diags, tiles, *got, *meta]
            if step >= COLORS:
                ins.append(sols[c])
            sol, change, *sends = call(
                functools.partial(step_kernel, plan, step),
                f"step{step}",
                ins,
                [SMEM],
                [sol_t, change_t] + plan.types(step),
            )
            sols[c:] = [sol] + sols[c + 1 :]
        last = step == steps - 1
        ins = [table, resid, tiles, change]
        if step > 0:
            ins += [*got, *meta]
        if last:
            ins += sols
        resid, *rest = call(
            functools.partial(local_kernel, plan, step, last),
            f"local{step}",
            ins,
            [SMEM],
            [resid_t] + ([jax.ShapeDtypeStruct(rhs.shape, f32)] if last else []),
            input_output_aliases={1: 0},
        )
        got = exchange(sends)
        if step == 0:
            meta = got
    (defect,) = call(
        functools.partial(final_kernel, plan, steps - 1),
        "final",
        [resid, *got, *meta],
        [],
        [jax.ShapeDtypeStruct(rhs.shape, f32)],
        out_specs=[HBM],
        scratch_shapes=[pltpu.VMEM(rhs.shape, f32), pltpu.SemaphoreType.DMA((rows,))],
    )
    return rest[0], defect


def solution(mesh):
    placed = (
        P(("dom", "sub"), None, None, None),
        P(("dom", "sub"), None, None),
        P(("dom", "sub"), None, None),
        P(("dom", "sub")),
        P(("dom", "sub"), None),
        P(("dom", "sub"), None),
        P(("dom", "sub"), None, None),
        P(("dom", "sub"), None),
    )
    return jax.shard_map(
        on_device,
        mesh=mesh,
        in_specs=placed,
        out_specs=(P(("dom", "sub"), None, None), P(("dom", "sub"), None, None)),
        check_vma=False,
    )
```
